128 devices in a mesh: seq: 32 (over x, y_hi, z), head: 4 (over y_lo, core).
Axes of the slice: x: 4, y: 4 (y_hi: 2, y_lo: 2; y = y_hi * 2 + y_lo), z: 4, core: 2. Of those that a mesh axis runs over, the one named last changes fastest.
Arguments:
- queries: bfloat16 [1024, 8192], P('seq', 'head'), may hold values from -20 to 20
- new_keys: bfloat16 [1024, 512], P('seq', 'head'), may hold values from -6 to 6
- new_values: bfloat16 [1024, 512], P('seq', 'head'), may hold values from -6 to 6
- cache_keys: bfloat16 [65536, 512], P('seq', 'head'), may hold values from -20 to 20
- cache_values: bfloat16 [65536, 512], P('seq', 'head'), may hold values from -6 to 6
- cache_lengths: int32 [32], P('seq'), may hold values from 1 to 2048, 32768 in all
- positions: int32 [1024], P('seq'), may hold values from 0 to 1023, each once
- out_weight: bfloat16 [8192, 16384], P('head', 'seq'), may hold values from -0.0625 to 0.0625
Outputs:
- projected: bfloat16 [1024, 16384], P(None, ('seq', 'head'))
The draws below stay inside these ranges and needn't reach their ends.
Inputs may be any that keep to these rules, and one draw needn't show every extreme that they name: The follow-up block's positions, each of 0 .. 1023 once. `cache_lengths`: the blocks' lengths sum to 32768; the longest block is full.
All inputs are finite; a program needn't handle non-finite values.
Results may differ from the reference program's by a relative error of at most 0.0063.
Values may be sent and summed in bfloat16 or wider, within the bound.
No kernel may reach another device: no remote copies, remote signals or barrier semaphores. Data moves between devices by JAX's collectives and lax.ppermute only.
A program may use at most 128 MiB of HBM per device.

```python
import math
import jax
import jax.numpy as jnp
import numpy as np
from jax import lax

D = 16384
HEADS = 64
KV_HEADS = 4
HD = 128
Q_DEV = 32
CACHE_DEV = 2048
Q_TOK = 1024
CACHE = 65536
N_SEQ = 32


def draw_queries(key, part):
    key = jax.random.fold_in(key, 11)
    result = jnp.clip(jax.random.normal(key, (Q_TOK, HEADS * HD), jnp.float32), -6.0, 6.0)
    return result.astype(jnp.bfloat16)


def draw_cache_keys(key, part):
    key = jax.random.fold_in(key, 12)
    result = jnp.clip(jax.random.normal(key, (CACHE, KV_HEADS * HD), jnp.float32), -6.0, 6.0)
    return result.astype(jnp.bfloat16)


def levels(key, shape, pieces, smallest, high):
    level = 1.0
    for dim, shards_of in pieces:
        draws = jax.random.uniform(jax.random.fold_in(jax.random.fold_in(key, 6), dim), (shards_of,), jnp.float32, smallest / len(pieces), high / len(pieces))
        level = level * jnp.repeat(jnp.exp(draws), shape[dim] // shards_of).reshape((-1,) + (1,) * (len(shape) - 1 - dim))
    return level


def length_profile(amount, total, reach, slope):
    portions = [(1 << 20) // math.isqrt(rank ** slope) + 1 for rank in range(2, amount + 1)]
    surplus, holding = total - reach - (amount - 1), [1] * (amount - 1)
    while surplus > 0:
        candidates = [i for i in range(amount - 1) if holding[i] < reach]
        whole, remaining = sum([portions[i] for i in candidates]), surplus
        for i in candidates:
            extra = min(reach - holding[i], max(1, remaining * portions[i] // whole), surplus)
            holding[i] = holding[i] + extra
            surplus = surplus - extra
    return np.array([reach] + holding)


def uneven(stream_key, count, total, bound, lean):
    if count == 2:
        one = jax.random.randint(stream_key, (), max(1, total - bound), min(bound, total - 1) + 1)
        return jnp.stack([one, total - one])
    lengths = jnp.asarray(length_profile(count, total, bound, lean), jnp.int32)
    couples = (count - 1) // 2
    donor, sink = lengths[1:1 + 2 * couples:2], lengths[2:2 + 2 * couples:2]
    slack = jnp.minimum(donor - 1, bound - sink)
    shifted = jax.random.randint(jax.random.fold_in(stream_key, 1), (couples,), 0, 1 << 20) % (slack + 1)
    lengths = lengths.at[1:1 + 2 * couples:2].set(donor - shifted).at[2:2 + 2 * couples:2].set(sink + shifted)
    return lengths[jax.random.permutation(jax.random.fold_in(stream_key, 2), count)]


def scatter_about(key, extent, scale, most, pieces=(), held_as=jnp.bfloat16):
    values = jax.random.normal(key, extent, jnp.float32) * scale
    if len(pieces) > 0:
        values = levels(key, extent, pieces, -0.22, 0.18) * values
    return jnp.clip(values, min=-most, max=most).astype(held_as)


def setup_inputs(seed: int = 0) -> dict:
    key_of = jax.random.split(jax.random.key(seed), 9)
    return {
        "queries": draw_queries(jax.random.fold_in(key_of[8], 71), 0),
        "new_keys": scatter_about(key_of[1], (Q_TOK, KV_HEADS * HD), 1.0, 6.0, ((0, 32), (1, 4))),
        "new_values": scatter_about(key_of[2], (Q_TOK, KV_HEADS * HD), 1.0, 6.0, ((0, 32), (1, 4))),
        "cache_keys": draw_cache_keys(jax.random.fold_in(key_of[8], 71), 0),
        "cache_values": scatter_about(key_of[4], (CACHE, KV_HEADS * HD), 1.0, 6.0, ((0, 32), (1, 4))),
        "cache_lengths": uneven(key_of[5], N_SEQ, N_SEQ * CACHE_DEV // 2, CACHE_DEV, 2).astype(jnp.int32),
        "positions": jax.random.permutation(key_of[6], Q_TOK).astype(jnp.int32),
        "out_weight": scatter_about(key_of[7], (HEADS * HD, D), (HEADS * HD) ** -0.5, 0.0625, ((0, 4), (1, 32))),
    }


def rank_partial(queries_f, positions, keys_block, values_block, new_positions, length):
    scale_factor = 1.0 / math.sqrt(HD)
    slot_ids = jnp.arange(CACHE_DEV, dtype=jnp.int32)
    cached_seen = jnp.broadcast_to(slot_ids[None, :] < length, (Q_TOK, CACHE_DEV))
    fresh_seen = new_positions[None, :] <= positions[:, None]
    visible = jnp.concatenate([cached_seen, fresh_seen], axis=1)
    outputs = []
    totals = []
    for head_group in range(KV_HEADS):
        scores = jnp.einsum('qjd,kd->jqk', queries_f[:, head_group], keys_block[:, head_group].astype(jnp.float32)) * scale_factor
        masked = jnp.where(visible[None], scores, -jnp.inf)
        largest = lax.optimization_barrier(jnp.max(masked, axis=-1))
        weights = jnp.where(visible[None], jnp.exp(scores - largest[..., None]), 0.0)
        total = lax.optimization_barrier(jnp.sum(weights, axis=-1))
        rounded = lax.optimization_barrier(weights.astype(jnp.bfloat16))
        summed = jnp.einsum('jqk,kd->qjd', rounded.astype(jnp.float32), values_block[:, head_group].astype(jnp.float32))
        partial_out = (summed / jnp.transpose(total)[..., None]).astype(jnp.bfloat16)
        outputs.append(partial_out)
        totals.append(jnp.transpose(largest + jnp.log(total)))
    return (jnp.concatenate(outputs, axis=1), jnp.concatenate(totals, axis=1))

def reference(queries, new_keys, new_values, cache_keys, cache_values, cache_lengths, positions, out_weight):
    group = HEADS // KV_HEADS
    queries_f = queries.astype(jnp.float32).reshape(Q_TOK, KV_HEADS, group, HD)
    keys_all = jnp.concatenate([cache_keys.reshape(N_SEQ, CACHE_DEV, KV_HEADS, HD), new_keys.reshape(N_SEQ, Q_DEV, KV_HEADS, HD)], axis=1)
    values_all = jnp.concatenate([cache_values.reshape(N_SEQ, CACHE_DEV, KV_HEADS, HD), new_values.reshape(N_SEQ, Q_DEV, KV_HEADS, HD)], axis=1)
    fresh = positions.reshape(N_SEQ, Q_DEV)

    def combine(carry, items):
        running_max, numer, denom = carry
        keys_block, values_block, new_positions, length = items
        partial_out, log_total = rank_partial(queries_f, positions, keys_block, values_block, new_positions, length)
        new_max = jnp.maximum(running_max, log_total)
        keep = jnp.exp(running_max - new_max)
        fresh_weight = jnp.exp(log_total - new_max)
        numer = numer * keep[..., None] + fresh_weight[..., None] * partial_out.astype(jnp.float32)
        denom = denom * keep + fresh_weight
        return ((new_max, numer, denom), log_total)
    start = (jnp.full((Q_TOK, HEADS), -1e+30, jnp.float32), jnp.zeros((Q_TOK, HEADS, HD), jnp.float32), jnp.zeros((Q_TOK, HEADS), jnp.float32))
    final_carry, stacked = lax.scan(combine, start, (keys_all, values_all, fresh, cache_lengths))
    numer = final_carry[1]
    denom = final_carry[2]
    attended = (numer / denom[..., None]).astype(jnp.bfloat16).reshape(Q_TOK, HEADS * HD)
    return jnp.dot(attended, out_weight, preferred_element_type=jnp.float32).astype(jnp.bfloat16)
```

```python
import functools
import math

import jax
import jax.numpy as jnp
from jax import lax
from jax.experimental import pallas as pl
from jax.experimental.pallas import tpu as pltpu
from jax.sharding import PartitionSpec as P

HD = 128
NX, NY, NZ = 4, 2, 4
SLOTS = 2048
TOK = 32
HEADS = 16
HALF = (HEADS // NY) * HD
PAY = HALF + HD
STEP_HEADS = 4
NEW0 = SLOTS
META0 = SLOTS + TOK
ROWS = META0 + 16
CUT = 1024
SUB = 128
CHUNK = 2048
TEMPER = math.log2(math.e) / math.sqrt(HD)
MIB = 2**20
BF16, F32 = jnp.bfloat16, jnp.float32


def seq_of(x, y, z):
    return ((x % NX) * NY + y % NY) * NZ + z % NZ


def shift(value, dx=0, dy=0, dz=0):
    perm = [
        (seq_of(x, y, z), seq_of(x + dx, y + dy, z + dz))
        for x in range(NX)
        for y in range(NY)
        for z in range(NZ)
    ]
    return lax.ppermute(value, "seq", perm)


def attend_kernel(y_ref, q_ref, asked_ref, kv0, kv1, kv2, kv3a, kv3b, *rest):
    del y_ref
    outs, (kt, v1, knt, vn1, seen, stats, info) = rest[:8], rest[8:]
    tokens = q_ref.shape[0]
    half, quarter = pl.program_id(0), pl.program_id(1)
    per = CHUNK // SUB
    lane = lax.broadcasted_iota(jnp.int32, (1, HD), 1)

    @pl.when((half == 0) & (quarter == 0))
    def _():
        offset = jnp.int32(0)
        fresh = jnp.zeros((1, HD), F32)
        for which, (tail, base) in enumerate(((kv0, 0), (kv1, 0), (kv2, 0), (kv3b, CUT))):
            meta = tail[META0 - base:META0 - base + 16, :].astype(F32)
            fresh = jnp.where(lane // TOK == which, meta[0:1, :HD] * 32.0 + meta[0:1, HD:], fresh)
            length = (jnp.max(meta[1:2, :HD]) * 64.0 + jnp.max(meta[1:2, HD:])).astype(jnp.int32)
            count = (length + SUB - 1) // SUB

            def put(i, source, begin, offset=offset, length=length):
                to = pl.multiple_of((offset + i) * SUB, SUB)
                block = source[pl.ds(pl.multiple_of(i * SUB - begin, SUB), SUB), :]
                kt[:, pl.ds(to, SUB)] = block[:, :HD].T
                v1[pl.ds(to, SUB), :HD] = block[:, HD:]
                rows = lax.broadcasted_iota(jnp.int32, (SUB, HD), 0) + i * SUB
                v1[pl.ds(to, SUB), HD:] = jnp.where(rows < length, 1.0, 0.0).astype(BF16)
                return 0

            if which < 3:
                lax.fori_loop(0, count, lambda i, _, tail=tail, put=put: put(i, tail, 0), 0)
            else:
                split = CUT // SUB
                lax.fori_loop(
                    0, jnp.minimum(count, split), lambda i, _, put=put: put(i, kv3a, 0), 0)
                lax.fori_loop(split, count, lambda i, _, put=put: put(i, kv3b, CUT), 0)
            offset = offset + count
            block = tail[NEW0 - base:NEW0 - base + TOK, :]
            knt[:, which * TOK:(which + 1) * TOK] = block[:, :HD].T
            vn1[which * TOK:(which + 1) * TOK, :HD] = block[:, HD:]
        vn1[:, HD:] = jnp.ones((4 * TOK, HD), BF16)
        loops = (offset + per - 1) // per

        def pad(i, _):
            to = pl.multiple_of(i * SUB, SUB)
            kt[:, pl.ds(to, SUB)] = kt[:, 0:SUB]
            v1[pl.ds(to, SUB), :] = jnp.zeros((SUB, 2 * HD), BF16)
            return 0

        lax.fori_loop(offset, loops * per, pad, 0)
        info[0] = loops
        asked = asked_ref[...].astype(F32)
        asked = asked[:, 0:1] * 32.0 + asked[:, 1:2]
        seen[...] = jnp.where(fresh <= asked, 1.0, 0.0)

    @pl.when(quarter == 0)
    def _():
        stats[...] = jnp.zeros_like(stats)

    visible = seen[...] > 0.0
    visible = jnp.concatenate([visible, visible], axis=0)
    queries, carry = [], []
    for j in range(0, STEP_HEADS, 2):
        q = jnp.concatenate(
            [q_ref[:, j * HD:(j + 1) * HD], q_ref[:, (j + 1) * HD:(j + 2) * HD]], axis=0)
        s = jnp.dot(q, knt[...], preferred_element_type=F32)
        top = jnp.max(jnp.where(visible, s, -1e30), axis=1, keepdims=True)
        p = jnp.where(visible, jnp.exp2((s - top) * TEMPER), 0.0).astype(BF16)
        queries.append(q)
        carry.append((top, jnp.dot(p, vn1[...], preferred_element_type=F32)))

    def step(i, carry):
        at = pl.multiple_of(i * CHUNK, CHUNK)
        k, v = kt[:, pl.ds(at, CHUNK)], v1[pl.ds(at, CHUNK), :]
        scores = [jnp.dot(q, k, preferred_element_type=F32) for q in queries]
        after = []
        for s, (top, acc) in zip(scores, carry):
            new = jnp.maximum(top, jnp.max(s, axis=1, keepdims=True))
            p = jnp.exp2((s - new) * TEMPER).astype(BF16)
            keep = jnp.exp2((top - new) * TEMPER)
            after.append((new, acc * keep + jnp.dot(p, v, preferred_element_type=F32)))
        return tuple(after)

    carry = lax.fori_loop(0, info[0], step, tuple(carry))
    log_total = stats[...]
    columns = []
    for pair, (top, acc) in enumerate(carry):
        total = acc[:, HD:]
        part = (acc[:, :HD] / total).astype(BF16)
        level = top * TEMPER + jnp.log2(total)
        for j in range(2):
            columns.append(part[j * tokens:(j + 1) * tokens])
            head = quarter * STEP_HEADS + pair * 2 + j
            log_total = jnp.where(lane == head, level[j * tokens:(j + 1) * tokens], log_total)
    stats[...] = log_total
    begin = pl.multiple_of(quarter * STEP_HEADS * HD, STEP_HEADS * HD)
    for dy in range(2):
        @pl.when(half == dy)
        def _(dy=dy):
            for dz in range(NZ):
                rows = slice(dz * NY * TOK, (dz + 1) * NY * TOK)
                for j, column in enumerate(columns):
                    outs[dy * NZ + dz][:, pl.ds(begin + j * HD, HD)] = column[rows]

            @pl.when(quarter == HEADS // NY // STEP_HEADS - 1)
            def _():
                high = log_total.astype(BF16)
                rest1 = log_total - high.astype(F32)
                middle = rest1.astype(BF16)
                low = (rest1 - middle.astype(F32)).astype(BF16)
                for dz in range(NZ):
                    rows = slice(dz * NY * TOK, (dz + 1) * NY * TOK)
                    for k, term in enumerate((high, middle, low)):
                        outs[dy * NZ + dz][:, HALF + k * 8:HALF + (k + 1) * 8] = term[rows, :8]
                    outs[dy * NZ + dz][:, HALF + 24:] = jnp.zeros((NY * TOK, HD - 24), BF16)


def attend(y, queries, blocks):
    tokens = queries.shape[0]
    steps = HEADS // NY // STEP_HEADS
    whole = lambda array: pl.BlockSpec(array.shape, lambda h, i, y: (0, 0))
    piece = (NY * TOK, PAY)
    return pl.pallas_call(
        attend_kernel,
        grid_spec=pltpu.PrefetchScalarGridSpec(
            num_scalar_prefetch=1,
            grid=(NY, steps),
            in_specs=[
                pl.BlockSpec(
                    (tokens, STEP_HEADS * HD),
                    lambda h, i, y: (0, lax.rem(h + y[0], NY) * steps + i)),
                pl.BlockSpec((tokens, HD), lambda h, i, y: (0, HEADS)),
            ] + [whole(block) for block in blocks],
            out_specs=[pl.BlockSpec(piece, lambda h, i, y: (0, 0))] * 8,
            scratch_shapes=[
                pltpu.VMEM((HD, NX * SLOTS), BF16),
                pltpu.VMEM((NX * SLOTS, 2 * HD), BF16),
                pltpu.VMEM((HD, NX * TOK), BF16),
                pltpu.VMEM((NX * TOK, 2 * HD), BF16),
                pltpu.VMEM((tokens, HD), F32),
                pltpu.VMEM((tokens, HD), F32),
                pltpu.SMEM((1,), jnp.int32),
            ],
        ),
        out_shape=[jax.ShapeDtypeStruct(piece, BF16)] * 8,
        compiler_params=pltpu.CompilerParams(vmem_limit_bytes=56 * MIB),
    )(y, queries, queries, *blocks)


def merge_kernel(y_ref, *refs):
    pieces, out = refs[:8], refs[8]
    y = y_ref[0]
    for other in range(2):
        def rows(dy):
            begin = TOK * (other ^ dy)
            return slice(begin, begin + TOK)

        sources = [(pieces[dy * NZ + dz], rows(dy)) for dy in range(2) for dz in range(NZ)]
        levels = []
        for ref, span in sources:
            split = ref[span, HALF:HALF + HD].astype(F32)
            levels.append(split[:, 0:8] + split[:, 8:16] + split[:, 16:24])
        top = functools.reduce(jnp.maximum, levels)
        shares = [jnp.exp2(level - top) for level in levels]
        whole = functools.reduce(jnp.add, shares)
        shares = [share / whole for share in shares]
        at = pl.multiple_of(lax.rem(y + other, 2) * TOK, TOK)
        for j in range(8):
            total = jnp.zeros((TOK, HD), F32)
            for (ref, span), share in zip(sources, shares):
                total += share[:, j:j + 1] * ref[span, j * HD:(j + 1) * HD].astype(F32)
            out[pl.ds(at, TOK), j * HD:(j + 1) * HD] = total.astype(BF16)


def merge(y, pieces):
    return pl.pallas_call(
        merge_kernel,
        in_specs=[pl.BlockSpec(memory_space=pltpu.SMEM)]
        + [pl.BlockSpec(memory_space=pltpu.VMEM)] * 8,
        out_specs=pl.BlockSpec(memory_space=pltpu.VMEM),
        out_shape=jax.ShapeDtypeStruct((NY * TOK, HALF), BF16),
        compiler_params=pltpu.CompilerParams(vmem_limit_bytes=32 * MIB),
    )(y, *pieces)


def place_kernel(x_ref, z_ref, own, first, second, third, out):
    total = own[...] + first[...].astype(F32) + second[...].astype(F32) + third[...].astype(F32)
    total = total.astype(BF16)
    for ya in range(NY):
        for dx in range(NX):
            for dz in range(NZ):
                begin = ((ya * NX + dx) * NZ + dz) * TOK
                x, z = lax.rem(x_ref[0] + dx, NX), lax.rem(z_ref[0] + dz, NZ)
                to = pl.multiple_of(((x * NY + ya) * NZ + z) * TOK, TOK)
                out[pl.ds(to, TOK), :] = total[begin:begin + TOK]


def place(x, z, own, received):
    return pl.pallas_call(
        place_kernel,
        in_specs=[pl.BlockSpec(memory_space=pltpu.SMEM)] * 2
        + [pl.BlockSpec(memory_space=pltpu.VMEM)] * 4,
        out_specs=pl.BlockSpec(memory_space=pltpu.VMEM),
        out_shape=jax.ShapeDtypeStruct(own.shape, BF16),
        compiler_params=pltpu.CompilerParams(vmem_limit_bytes=32 * MIB),
    )(x, z, own, *received)


def ring(value, axis):
    ahead, behind = {axis: 1}, {axis: -1}
    before = shift(value, **ahead)
    after = shift(value, **behind)
    middle = value.shape[0] // 2
    across = jnp.concatenate(
        [shift(before[:middle], **ahead), shift(after[middle:], **behind)], axis=0)
    return [value, after, across, before]


def gather(value, first, second):
    quarter = value.shape[0]
    line = jnp.concatenate(ring(value, first), axis=0)
    plane = jnp.stack(ring(line, second), axis=0).reshape(4, 4, quarter, -1)
    return plane if second == "dx" else jnp.swapaxes(plane, 0, 1)


def per_device(
    queries, new_keys, new_values, cache_keys, cache_values, cache_lengths, positions, out_weight
):
    me = lax.axis_index("seq")
    x, y, z = me // (NY * NZ), me // NZ % NY, me % NZ
    head = lax.axis_index("head")
    scalar = lambda value: jnp.asarray(value, jnp.int32).reshape(1)

    length = cache_lengths[0]
    used = jnp.arange(SLOTS, dtype=jnp.int32)[:, None] < length
    keys = jnp.where(used, cache_keys, cache_keys[0:1])
    values = jnp.where(used, cache_values, jnp.zeros((), BF16))
    high, low = (positions // 32).astype(BF16), (positions % 32).astype(BF16)
    meta = jnp.concatenate([
        jnp.concatenate([jnp.tile(high, 4), jnp.tile(low, 4)])[None],
        jnp.concatenate([
            jnp.full((1, HD), (length // 64).astype(BF16)),
            jnp.full((1, HD), (length % 64).astype(BF16))], axis=1),
        jnp.zeros((14, 2 * HD), BF16)], axis=0)
    block = jnp.concatenate([
        jnp.concatenate([keys, values], axis=1),
        jnp.concatenate([new_keys, new_values], axis=1), meta], axis=0)
    asking = jnp.concatenate(
        [queries, high[:, None], low[:, None], jnp.zeros((TOK, HD - 2), BF16)], axis=1)

    before, after = shift(block, dx=1), shift(block, dx=-1)
    across = (shift(before[:CUT], dx=1), shift(after[CUT:], dx=-1))
    asked = jnp.concatenate(
        [asking if (dy, dz) == (0, 0) else shift(asking, dy=dy, dz=-dz)
         for dz in range(NZ) for dy in range(NY)], axis=0)
    partial = attend(scalar(y), asked, (block, before, after) + across)
    received = [
        partial[dy * NZ + dz] if (dy, dz) == (0, 0) else shift(partial[dy * NZ + dz], dy=dy, dz=dz)
        for dy in range(NY) for dz in range(NZ)]
    merged = merge(scalar(y), received)

    width = out_weight.shape[1]
    mine = lax.dynamic_slice_in_dim(out_weight, y * HALF, HALF)
    theirs = shift(lax.dynamic_slice_in_dim(out_weight, (1 - y) * HALF, HALF), dy=1)
    low_y, core = head // 2, head % 2

    def columns(weight, dlow, dcore):
        other = (low_y + dlow) % 2 * 2 + (core + dcore) % 2
        return lax.dynamic_slice_in_dim(weight, other * HD, HD, axis=1)

    weight = jnp.concatenate([
        columns(source, dlow, dcore)
        for dcore in range(2) for source in (mine, theirs) for dlow in range(2)], axis=1)

    rows = jnp.concatenate([
        gather(merged[:TOK], "dz", "dx").reshape(-1, HALF),
        gather(merged[TOK:], "dx", "dz").reshape(-1, HALF)], axis=0)
    terms = jnp.dot(rows, weight, preferred_element_type=F32)
    to_core = lax.ppermute(
        terms[:, width:].astype(BF16), "head", [(h, h ^ 1) for h in range(4)])
    terms = terms[:, :width] + to_core.astype(F32)

    def across_y(value, dy, dlow):
        perm = [
            ((s * 4 + h), (s ^ (dy * NZ)) * 4 + (h ^ (dlow * 2)))
            for s in range(NX * NY * NZ) for h in range(4)]
        return lax.ppermute(value, ("seq", "head"), perm)

    others = [
        across_y(terms[:, k * HD:(k + 1) * HD].astype(BF16), k // 2, k % 2) for k in range(1, 4)]
    return place(scalar(x), scalar(z), terms[:, :HD], others)


def solution(mesh):
    return jax.shard_map(
        per_device,
        mesh=mesh,
        in_specs=(
            P("seq", "head"),
            P("seq", "head"),
            P("seq", "head"),
            P("seq", "head"),
            P("seq", "head"),
            P("seq"),
            P("seq"),
            P("head", "seq"),
        ),
        out_specs=P(None, ("seq", "head")),
        check_vma=False,
    )
```

```python
import functools
import math

import jax
import jax.numpy as jnp
from jax import lax
from jax.experimental import pallas as pl
from jax.experimental.pallas import tpu as pltpu
from jax.sharding import PartitionSpec as P

HD = 128
NX, NY, NZ = 4, 2, 4
SLOTS = 2048
TOK = 32
HEADS = 16
HALF = (HEADS // NY) * HD
PAY = HALF + HD
GROUP = NY * NZ * TOK
PAIRS = HEADS // 2
LANES = 2 * GROUP
DEPTH = HD + 16
NEW0 = SLOTS
META0 = SLOTS + TOK
CUT = 1024
CHUNK = 512
HEADROOM = 60.0
TEMPER = math.log2(math.e) / math.sqrt(HD)
MIB = 2**20
BF16, F32 = jnp.bfloat16, jnp.float32


def seq_of(x, y, z):
    return ((x % NX) * NY + y % NY) * NZ + z % NZ


PLANES_YZ = [[seq_of(x, y, z) for y in range(NY) for z in range(NZ)] for x in range(NX)]
PLANES_XZ = [[seq_of(x, y, z) for x in range(NX) for z in range(NZ)] for y in range(NY)]


def swap(value, groups):
    return lax.all_to_all(value, "seq", 0, 0, axis_index_groups=groups, tiled=True)


def shift(value, dx=0, dy=0, dz=0):
    perm = [
        (seq_of(x, y, z), seq_of(x + dx, y + dy, z + dz))
        for x in range(NX)
        for y in range(NY)
        for z in range(NZ)
    ]
    return lax.ppermute(value, "seq", perm)


def attend_kernel(first, last, spans, q_ref, *rest):
    rest = list(rest)
    take = lambda n: [rest.pop(0) for _ in range(n)]
    asked_ref = take(1)[0] if last else None
    fresh_refs = take(4) if last else []
    refs = take(len(spans))
    top_in, acc_in = (None, None) if first else take(2)
    out_refs = take(1) if last else take(2)
    top_ref, acc_ref = take(2) if last else out_refs
    high_ref = take(1)[0]

    def length_of(ref, base):
        meta = ref[META0 - base:META0 - base + 16, :].astype(F32)
        return (jnp.max(meta[:, 2:3]) * 64.0 + jnp.max(meta[:, 3:4])).astype(jnp.int32)

    def queries(pair):
        return jnp.concatenate(
            [q_ref[:, (2 * pair + j) * HD:(2 * pair + j + 1) * HD] for j in range(2)], axis=0)

    def score(keys, pair):
        return lax.dot_general(
            keys, queries(pair), (((1,), (1,)), ((), ())), preferred_element_type=F32)

    def chunk_of(ref, base, length, i):
        at = pl.multiple_of(i * CHUNK - base, CHUNK)
        block = ref[pl.ds(at, CHUNK), :]
        slot = lax.broadcasted_iota(jnp.int32, (DEPTH - HD, CHUNK), 1) + i * CHUNK
        ones = jnp.where(slot < length, 1.0, 0.0).astype(BF16)
        return block[:, :HD], jnp.concatenate([block[:, HD:].T, ones], axis=0)

    def eights(s):
        return jnp.max(s.reshape(s.shape[0] // 8, 8, LANES), axis=0)

    if last:
        news = [ref[NEW0 - base:NEW0 - base + TOK, :] for ref, base in zip(fresh_refs, (0, 0, 0, CUT))]
        news = jnp.concatenate(news, axis=0)
        new_keys = news[:, :HD]
        new_values = jnp.concatenate(
            [news[:, HD:].T, jnp.ones((DEPTH - HD, NX * TOK), BF16)], axis=0)
        metas = [ref[META0 - base:META0 - base + TOK, :] for ref, base in zip(fresh_refs, (0, 0, 0, CUT))]
        metas = jnp.concatenate(metas, axis=0).astype(F32)
        given = metas[:, 0:1] * 32.0 + metas[:, 1:2]
        asked = asked_ref[...].astype(F32).T
        asked = asked[0:1] * 32.0 + asked[1:2]
        visible = given <= asked
        visible = jnp.concatenate([visible, visible], axis=1)

    lengths = [length_of(ref, base) for ref, base in spans_of(spans, refs, fresh_refs)]

    def loops(body):
        for ref, (base, slots, _), length in zip(refs, spans, lengths):
            begin, end = base // CHUNK, (base + slots) // CHUNK
            stop = jnp.minimum((length + CHUNK - 1) // CHUNK, end)

            def once(i, _, ref=ref, base=base, length=length):
                body(*chunk_of(ref, base, length, i))
                return 0

            lax.fori_loop(begin, stop, once, 0)

    for pair in range(PAIRS):
        if first:
            top_ref[pair] = jnp.max(score(refs[0][0:CHUNK, :HD], pair), axis=0, keepdims=True)
            acc_ref[pair] = jnp.zeros((DEPTH, LANES), F32)
        else:
            top_ref[pair] = top_in[pair]
            acc_ref[pair] = acc_in[pair]
        high_ref[pair] = jnp.full((8, LANES), -1e30, F32)

    def add(keys, values):
        scores = [score(keys, pair) for pair in range(PAIRS)]
        for pair, s in enumerate(scores):
            high_ref[pair] = jnp.maximum(high_ref[pair], eights(s))
            p = jnp.exp2((s - top_ref[pair]) * TEMPER).astype(BF16)
            acc_ref[pair] += jnp.dot(values, p, preferred_element_type=F32)

    loops(add)
    if last:
        for pair in range(PAIRS):
            s = score(new_keys, pair)
            high_ref[pair] = jnp.maximum(high_ref[pair], eights(jnp.where(visible, s, -1e30)))
            p = jnp.where(visible, jnp.exp2((s - top_ref[pair]) * TEMPER), 0.0).astype(BF16)
            acc_ref[pair] += jnp.dot(new_values, p, preferred_element_type=F32)
    excess = functools.reduce(
        jnp.maximum, [high_ref[pair] - top_ref[pair] for pair in range(PAIRS)])

    @pl.when(jnp.max(excess) * TEMPER > HEADROOM)
    def _():
        for pair in range(PAIRS):
            top_ref[pair] = jnp.full((1, LANES), -1e30, F32) if first else top_in[pair]
            acc_ref[pair] = jnp.zeros((DEPTH, LANES), F32) if first else acc_in[pair]

        def raised(pair, s, values, seen):
            shown = s if seen is None else jnp.where(seen, s, -1e30)
            new = jnp.maximum(top_ref[pair], jnp.max(shown, axis=0, keepdims=True))
            p = jnp.exp2((s - new) * TEMPER)
            p = (p if seen is None else jnp.where(seen, p, 0.0)).astype(BF16)
            keep = jnp.exp2((top_ref[pair] - new) * TEMPER)
            acc_ref[pair] = acc_ref[pair] * keep + jnp.dot(values, p, preferred_element_type=F32)
            top_ref[pair] = new

        def careful(keys, values):
            for pair in range(PAIRS):
                raised(pair, score(keys, pair), values, None)

        loops(careful)
        if last:
            for pair in range(PAIRS):
                raised(pair, score(new_keys, pair), new_values, visible)

    if last:
        out = out_refs[0]
        for half in range(NY):
            levels = []
            for pair in range(half * PAIRS // 2, (half + 1) * PAIRS // 2):
                total = acc_ref[pair, HD:HD + 1, :]
                level = top_ref[pair] * TEMPER + jnp.log2(total)
                part = acc_ref[pair, :HD, :] / total
                for j in range(2):
                    levels.append(level[:, j * GROUP:(j + 1) * GROUP])
                    block = part[:, j * GROUP:(j + 1) * GROUP].T.astype(BF16)
                    at = (2 * pair + j) * HD - half * HALF
                    for z in range(NZ):
                        for y in range(NY):
                            rows = y * NZ * TOK + z * TOK
                            out[half * NZ + z, y * TOK:(y + 1) * TOK, at:at + HD] = (
                                block[rows:rows + TOK])
            level = jnp.concatenate(levels, axis=0)
            high = level.astype(BF16).astype(F32)
            middle = (level - high).astype(BF16).astype(F32)
            low = level - high - middle
            block = jnp.concatenate(
                [high, middle, low, jnp.zeros((HD - 24, GROUP), F32)], axis=0).T.astype(BF16)
            for z in range(NZ):
                for y in range(NY):
                    rows = y * NZ * TOK + z * TOK
                    out[half * NZ + z, y * TOK:(y + 1) * TOK, HALF:] = block[rows:rows + TOK]


def spans_of(spans, refs, fresh_refs):
    for ref, (base, _, holder) in zip(refs, spans):
        yield (ref, base) if holder is None else (fresh_refs[holder], CUT)


def attend(asked, blocks, spans, state=None, fresh=None):
    first, last = state is None, fresh is not None
    operands = [asked] + ([asked] + list(fresh) if last else []) + list(blocks) + list(state or ())
    whole = lambda array: pl.BlockSpec(array.shape, lambda i: (0,) * array.ndim)
    specs = [pl.BlockSpec((GROUP, HEADS * HD), lambda i: (0, 0))]
    if last:
        specs += [pl.BlockSpec((GROUP, HD), lambda i: (0, HEADS))]
    specs += [whole(operand) for operand in operands[len(specs):]]
    held = [
        jax.ShapeDtypeStruct((PAIRS, 1, LANES), F32),
        jax.ShapeDtypeStruct((PAIRS, DEPTH, LANES), F32)]
    results = [jax.ShapeDtypeStruct((NY * NZ, NY * TOK, PAY), BF16)] if last else held
    scratch = [pltpu.VMEM(h.shape, F32) for h in held] if last else []
    keys = sum(slots for _, slots, _ in spans)
    out = pl.pallas_call(
        functools.partial(attend_kernel, first, last, spans),
        grid=(1,),
        in_specs=specs,
        out_specs=[whole(result) for result in results],
        out_shape=results,
        scratch_shapes=scratch + [pltpu.VMEM((PAIRS, 8, LANES), F32)],
        cost_estimate=pl.CostEstimate(
            flops=4 * HEADS * GROUP * HD * keys, transcendentals=HEADS * GROUP * keys,
            bytes_accessed=4 * MIB),
        compiler_params=pltpu.CompilerParams(vmem_limit_bytes=60 * MIB),
    )(*operands)
    return out[0] if last else out


def merge_kernel(pieces, out):
    count = NY * NZ
    split = [pieces[r, :, HALF:].astype(F32) for r in range(count)]
    levels = [term[:, 0:8] + term[:, 8:16] + term[:, 16:24] for term in split]
    top = functools.reduce(jnp.maximum, levels)
    shares = [jnp.exp2(level - top) for level in levels]
    whole = functools.reduce(jnp.add, shares)
    for j in range(HALF // HD):
        total = jnp.zeros((NY * TOK, HD), F32)
        for r in range(count):
            total += shares[r][:, j:j + 1] * pieces[r, :, j * HD:(j + 1) * HD].astype(F32)
        merged = (total / whole[:, j:j + 1]).astype(BF16)
        for to in range(NX * NZ):
            out[to, :, j * HD:(j + 1) * HD] = merged


def merge(pieces):
    return pl.pallas_call(
        merge_kernel,
        in_specs=[pl.BlockSpec(memory_space=pltpu.VMEM)],
        out_specs=pl.BlockSpec(memory_space=pltpu.VMEM),
        out_shape=jax.ShapeDtypeStruct((NX * NZ, NY * TOK, HALF), BF16),
        compiler_params=pltpu.CompilerParams(vmem_limit_bytes=32 * MIB),
    )(pieces)


def place_kernel(own, first, second, third, out):
    total = own[...] + first[...].astype(F32) + second[...].astype(F32) + third[...].astype(F32)
    total = total.astype(BF16)
    for x in range(NX):
        for z in range(NZ):
            for y in range(NY):
                begin = ((x * NZ + z) * NY + y) * TOK
                to = seq_of(x, y, z) * TOK
                out[to:to + TOK, :] = total[begin:begin + TOK]


def place(own, received):
    return pl.pallas_call(
        place_kernel,
        in_specs=[pl.BlockSpec(memory_space=pltpu.VMEM)] * 4,
        out_specs=pl.BlockSpec(memory_space=pltpu.VMEM),
        out_shape=jax.ShapeDtypeStruct(own.shape, BF16),
        compiler_params=pltpu.CompilerParams(vmem_limit_bytes=32 * MIB),
    )(own, *received)


def per_device(
    queries, new_keys, new_values, cache_keys, cache_values, cache_lengths, positions, out_weight
):
    y = lax.axis_index("seq") // NZ % NY
    head = lax.axis_index("head")

    length = cache_lengths[0]
    used = jnp.arange(SLOTS, dtype=jnp.int32)[:, None] < length
    keys = jnp.where(used, cache_keys, cache_keys[0:1])
    values = jnp.where(used, cache_values, jnp.zeros((), BF16))
    high, low = (positions // 32).astype(BF16), (positions % 32).astype(BF16)
    meta = jnp.concatenate([
        high[:, None], low[:, None],
        jnp.full((TOK, 1), (length // 64).astype(BF16)),
        jnp.full((TOK, 1), (length % 64).astype(BF16)),
        jnp.zeros((TOK, 2 * HD - 4), BF16)], axis=1)
    block = jnp.concatenate([
        jnp.concatenate([keys, values], axis=1),
        jnp.concatenate([new_keys, new_values], axis=1), meta], axis=0)
    asking = jnp.concatenate(
        [queries, high[:, None], low[:, None], jnp.zeros((TOK, HD - 2), BF16)], axis=1)

    asked = swap(jnp.broadcast_to(asking, (NY * NZ,) + asking.shape), PLANES_YZ)
    asked = asked.reshape(GROUP, asking.shape[1])
    before, after = shift(block, dx=1), shift(block, dx=-1)
    across = (shift(before[:CUT], dx=1), shift(after[CUT:], dx=-1))
    state = attend(asked, [block], ((0, SLOTS, None),))
    state = attend(asked, [before, after], ((0, SLOTS, None),) * 2, state)
    partial = attend(
        asked, across, ((0, CUT, 3), (CUT, SLOTS - CUT, 3)), state,
        (block, before, after, across[1]))
    merged = merge(swap(partial, PLANES_YZ))

    width = out_weight.shape[1]
    mine = lax.dynamic_slice_in_dim(out_weight, y * HALF, HALF)
    theirs = shift(lax.dynamic_slice_in_dim(out_weight, (1 - y) * HALF, HALF), dy=1)
    low_y, core = head // 2, head % 2

    def columns(weight, dlow, dcore):
        other = (low_y + dlow) % 2 * 2 + (core + dcore) % 2
        return lax.dynamic_slice_in_dim(weight, other * HD, HD, axis=1)

    weight = jnp.concatenate([
        columns(source, dlow, dcore)
        for dcore in range(2) for source in (mine, theirs) for dlow in range(2)], axis=1)

    rows = swap(merged, PLANES_XZ).reshape(-1, HALF)
    terms = jnp.dot(rows, weight, preferred_element_type=F32)
    to_core = lax.ppermute(
        terms[:, width:].astype(BF16), "head", [(h, h ^ 1) for h in range(4)])
    terms = terms[:, :width] + to_core.astype(F32)

    def across_y(value, dy, dlow):
        perm = [
            ((s * 4 + h), (s ^ (dy * NZ)) * 4 + (h ^ (dlow * 2)))
            for s in range(NX * NY * NZ) for h in range(4)]
        return lax.ppermute(value, ("seq", "head"), perm)

    others = [
        across_y(terms[:, k * HD:(k + 1) * HD].astype(BF16), k // 2, k % 2) for k in range(1, 4)]
    return place(terms[:, :HD], others)


def solution(mesh):
    return jax.shard_map(
        per_device,
        mesh=mesh,
        in_specs=(
            P("seq", "head"),
            P("seq", "head"),
            P("seq", "head"),
            P("seq", "head"),
            P("seq", "head"),
            P("seq"),
            P("seq"),
            P("head", "seq"),
        ),
        out_specs=P(None, ("seq", "head")),
        check_vma=False,
    )
```

```python
import functools
import math

import jax
import jax.numpy as jnp
from jax import lax
from jax.experimental import pallas as pl
from jax.experimental.pallas import tpu as pltpu
from jax.sharding import PartitionSpec as P

HD = 128
NX, NY, NZ = 4, 2, 4
SLOTS = 2048
TOK = 32
HEADS = 16
HALF = (HEADS // NY) * HD
PAY = HALF + HD
GROUP = NY * NZ * TOK
PAIRS = HEADS // 2
LANES = 2 * GROUP
DEPTH = HD + 16
NEW0 = SLOTS
META0 = SLOTS + TOK
CUT = 1024
CHUNK = 512
HEADROOM = 60.0
TEMPER = math.log2(math.e) / math.sqrt(HD)
MIB = 2**20
BF16, F32 = jnp.bfloat16, jnp.float32


def seq_of(x, y, z):
    return ((x % NX) * NY + y % NY) * NZ + z % NZ


PLANES_YZ = [[seq_of(x, y, z) for y in range(NY) for z in range(NZ)] for x in range(NX)]
PLANES_XZ = [[seq_of(x, y, z) for x in range(NX) for z in range(NZ)] for y in range(NY)]


def swap(value, groups):
    return lax.all_to_all(value, "seq", 0, 0, axis_index_groups=groups, tiled=True)


def shift(value, dx=0, dy=0, dz=0):
    perm = [
        (seq_of(x, y, z), seq_of(x + dx, y + dy, z + dz))
        for x in range(NX)
        for y in range(NY)
        for z in range(NZ)
    ]
    return lax.ppermute(value, "seq", perm)


def attend_kernel(first, last, spans, q_ref, *rest):
    rest = list(rest)
    take = lambda n: [rest.pop(0) for _ in range(n)]
    asked_ref = take(1)[0] if last else None
    fresh_refs = take(4) if last else []
    refs = take(len(spans))
    top_in, acc_in = (None, None) if first else take(2)
    out_refs = take(1) if last else take(2)
    top_ref, acc_ref = take(2) if last else out_refs
    high_ref = take(1)[0]

    def length_of(ref, base):
        meta = ref[META0 - base:META0 - base + 16, :].astype(F32)
        return (jnp.max(meta[:, 2:3]) * 64.0 + jnp.max(meta[:, 3:4])).astype(jnp.int32)

    def queries(pair):
        return jnp.concatenate(
            [q_ref[:, (2 * pair + j) * HD:(2 * pair + j + 1) * HD] for j in range(2)], axis=0)

    def score(keys, pair):
        return lax.dot_general(
            keys, queries(pair), (((1,), (1,)), ((), ())), preferred_element_type=F32)

    def chunk_of(ref, base, length, i):
        at = pl.multiple_of(i * CHUNK - base, CHUNK)
        block = ref[pl.ds(at, CHUNK), :]
        slot = lax.broadcasted_iota(jnp.int32, (DEPTH - HD, CHUNK), 1) + i * CHUNK
        ones = jnp.where(slot < length, 1.0, 0.0).astype(BF16)
        return block[:, :HD], jnp.concatenate([block[:, HD:].T, ones], axis=0)

    def eights(s):
        return jnp.max(s.reshape(s.shape[0] // 8, 8, LANES), axis=0)

    if last:
        news = [ref[NEW0 - base:NEW0 - base + TOK, :] for ref, base in zip(fresh_refs, (0, 0, 0, CUT))]
        news = jnp.concatenate(news, axis=0)
        new_keys = news[:, :HD]
        new_values = jnp.concatenate(
            [news[:, HD:].T, jnp.ones((DEPTH - HD, NX * TOK), BF16)], axis=0)
        metas = [ref[META0 - base:META0 - base + TOK, :] for ref, base in zip(fresh_refs, (0, 0, 0, CUT))]
        metas = jnp.concatenate(metas, axis=0).astype(F32)
        given = metas[:, 0:1] * 32.0 + metas[:, 1:2]
        asked = asked_ref[...].astype(F32).T
        asked = asked[0:1] * 32.0 + asked[1:2]
        visible = given <= asked
        visible = jnp.concatenate([visible, visible], axis=1)

    lengths = [length_of(ref, base) for ref, base in spans_of(spans, refs, fresh_refs)]

    def loops(body):
        for ref, (base, slots, _), length in zip(refs, spans, lengths):
            begin, end = base // CHUNK, (base + slots) // CHUNK
            stop = jnp.minimum((length + CHUNK - 1) // CHUNK, end)

            def once(i, _, ref=ref, base=base, length=length):
                body(*chunk_of(ref, base, length, i))
                return 0

            lax.fori_loop(begin, stop, once, 0)

    for pair in range(PAIRS):
        if first:
            top_ref[pair] = jnp.max(score(refs[0][0:CHUNK, :HD], pair), axis=0, keepdims=True)
            acc_ref[pair] = jnp.zeros((DEPTH, LANES), F32)
        else:
            top_ref[pair] = top_in[pair]
            acc_ref[pair] = acc_in[pair]
        high_ref[pair] = jnp.full((8, LANES), -1e30, F32)

    def add(keys, values):
        scores = [score(keys, pair) for pair in range(PAIRS)]
        for pair, s in enumerate(scores):
            high_ref[pair] = jnp.maximum(high_ref[pair], eights(s))
            p = jnp.exp2((s - top_ref[pair]) * TEMPER).astype(BF16)
            acc_ref[pair] += jnp.dot(values, p, preferred_element_type=F32)

    loops(add)
    if last:
        for pair in range(PAIRS):
            s = score(new_keys, pair)
            high_ref[pair] = jnp.maximum(high_ref[pair], eights(jnp.where(visible, s, -1e30)))
            p = jnp.where(visible, jnp.exp2((s - top_ref[pair]) * TEMPER), 0.0).astype(BF16)
            acc_ref[pair] += jnp.dot(new_values, p, preferred_element_type=F32)
    excess = functools.reduce(
        jnp.maximum, [high_ref[pair] - top_ref[pair] for pair in range(PAIRS)])

    @pl.when(jnp.max(excess) * TEMPER > HEADROOM)
    def _():
        for pair in range(PAIRS):
            top_ref[pair] = jnp.full((1, LANES), -1e30, F32) if first else top_in[pair]
            acc_ref[pair] = jnp.zeros((DEPTH, LANES), F32) if first else acc_in[pair]

        def raised(pair, s, values, seen):
            shown = s if seen is None else jnp.where(seen, s, -1e30)
            new = jnp.maximum(top_ref[pair], jnp.max(shown, axis=0, keepdims=True))
            p = jnp.exp2((s - new) * TEMPER)
            p = (p if seen is None else jnp.where(seen, p, 0.0)).astype(BF16)
            keep = jnp.exp2((top_ref[pair] - new) * TEMPER)
            acc_ref[pair] = acc_ref[pair] * keep + jnp.dot(values, p, preferred_element_type=F32)
            top_ref[pair] = new

        def careful(keys, values):
            for pair in range(PAIRS):
                raised(pair, score(keys, pair), values, None)

        loops(careful)
        if last:
            for pair in range(PAIRS):
                raised(pair, score(new_keys, pair), new_values, visible)

    if last:
        out = out_refs[0]
        for half in range(NY):
            levels = []
            for pair in range(half * PAIRS // 2, (half + 1) * PAIRS // 2):
                total = acc_ref[pair, HD:HD + 1, :]
                level = top_ref[pair] * TEMPER + jnp.log2(total)
                part = acc_ref[pair, :HD, :] / total
                for j in range(2):
                    levels.append(level[:, j * GROUP:(j + 1) * GROUP])
                    block = part[:, j * GROUP:(j + 1) * GROUP].T.astype(BF16)
                    at = (2 * pair + j) * HD - half * HALF
                    for z in range(NZ):
                        for y in range(NY):
                            rows = y * NZ * TOK + z * TOK
                            out[half * NZ + z, y * TOK:(y + 1) * TOK, at:at + HD] = (
                                block[rows:rows + TOK])
            level = jnp.concatenate(levels, axis=0)
            high = level.astype(BF16).astype(F32)
            middle = (level - high).astype(BF16).astype(F32)
            low = level - high - middle
            block = jnp.concatenate(
                [high, middle, low, jnp.zeros((HD - 24, GROUP), F32)], axis=0).T.astype(BF16)
            for z in range(NZ):
                for y in range(NY):
                    rows = y * NZ * TOK + z * TOK
                    out[half * NZ + z, y * TOK:(y + 1) * TOK, HALF:] = block[rows:rows + TOK]


def spans_of(spans, refs, fresh_refs):
    for ref, (base, _, holder) in zip(refs, spans):
        yield (ref, base) if holder is None else (fresh_refs[holder], CUT)


def attend(asked, blocks, spans, state=None, fresh=None):
    first, last = state is None, fresh is not None
    operands = [asked] + ([asked] + list(fresh) if last else []) + list(blocks) + list(state or ())
    whole = lambda array: pl.BlockSpec(array.shape, lambda i: (0,) * array.ndim)
    specs = [pl.BlockSpec((GROUP, HEADS * HD), lambda i: (0, 0))]
    if last:
        specs += [pl.BlockSpec((GROUP, HD), lambda i: (0, HEADS))]
    specs += [whole(operand) for operand in operands[len(specs):]]
    held = [
        jax.ShapeDtypeStruct((PAIRS, 1, LANES), F32),
        jax.ShapeDtypeStruct((PAIRS, DEPTH, LANES), F32)]
    results = [jax.ShapeDtypeStruct((NY * NZ, NY * TOK, PAY), BF16)] if last else held
    scratch = [pltpu.VMEM(h.shape, F32) for h in held] if last else []
    keys = sum(slots for _, slots, _ in spans)
    out = pl.pallas_call(
        functools.partial(attend_kernel, first, last, spans),
        grid=(1,),
        in_specs=specs,
        out_specs=[whole(result) for result in results],
        out_shape=results,
        scratch_shapes=scratch + [pltpu.VMEM((PAIRS, 8, LANES), F32)],
        cost_estimate=pl.CostEstimate(
            flops=4 * HEADS * GROUP * HD * keys, transcendentals=HEADS * GROUP * keys,
            bytes_accessed=4 * MIB),
        compiler_params=pltpu.CompilerParams(vmem_limit_bytes=60 * MIB),
    )(*operands)
    return out[0] if last else out


def merge_kernel(pieces, out):
    count = NY * NZ
    split = [pieces[r, :, HALF:].astype(F32) for r in range(count)]
    levels = [term[:, 0:8] + term[:, 8:16] + term[:, 16:24] for term in split]
    top = functools.reduce(jnp.maximum, levels)
    shares = [jnp.exp2(level - top) for level in levels]
    whole = functools.reduce(jnp.add, shares)
    for j in range(HALF // HD):
        total = jnp.zeros((NY * TOK, HD), F32)
        for r in range(count):
            total += shares[r][:, j:j + 1] * pieces[r, :, j * HD:(j + 1) * HD].astype(F32)
        merged = (total / whole[:, j:j + 1]).astype(BF16)
        for to in range(NX * NZ):
            out[to, :, j * HD:(j + 1) * HD] = merged


def merge(pieces):
    return pl.pallas_call(
        merge_kernel,
        in_specs=[pl.BlockSpec(memory_space=pltpu.VMEM)],
        out_specs=pl.BlockSpec(memory_space=pltpu.VMEM),
        out_shape=jax.ShapeDtypeStruct((NX * NZ, NY * TOK, HALF), BF16),
        compiler_params=pltpu.CompilerParams(vmem_limit_bytes=32 * MIB),
    )(pieces)


def project_kernel(at_ref, rows, mine, theirs, kept, sent):
    low_y, core = at_ref[1], at_ref[2]
    for dcore, out in ((0, kept), (1, sent)):
        for k, weight in enumerate((mine, theirs)):
            picked = []
            for dlow in range(2):
                head = lax.rem(low_y + dlow, 2) * 2 + lax.rem(core + dcore, 2)
                picked.append(weight[:, pl.ds(pl.multiple_of(head * HD, HD), HD)])
            terms = jnp.dot(
                rows[...], jnp.concatenate(picked, axis=1), preferred_element_type=F32)
            out[:, 2 * k * HD:2 * (k + 1) * HD] = terms.astype(out.dtype)


def project(at, rows, weight, theirs):
    count, width = rows.shape[0], theirs.shape[1]
    part = count // 4
    return pl.pallas_call(
        project_kernel,
        grid_spec=pltpu.PrefetchScalarGridSpec(
            num_scalar_prefetch=1,
            grid=(count // part,),
            in_specs=[
                pl.BlockSpec((part, HALF), lambda i, at: (i, 0)),
                pl.BlockSpec((HALF, width), lambda i, at: (at[0], 0)),
                pl.BlockSpec((HALF, width), lambda i, at: (0, 0)),
            ],
            out_specs=[pl.BlockSpec((part, width), lambda i, at: (i, 0))] * 2,
        ),
        out_shape=[
            jax.ShapeDtypeStruct((count, width), F32),
            jax.ShapeDtypeStruct((count, width), BF16)],
        compiler_params=pltpu.CompilerParams(vmem_limit_bytes=32 * MIB),
    )(at, rows, weight, theirs)


def place_kernel(own, first, second, third, out):
    total = own[...] + first[...].astype(F32) + second[...].astype(F32) + third[...].astype(F32)
    total = total.astype(BF16)
    for x in range(NX):
        for z in range(NZ):
            for y in range(NY):
                begin = ((x * NZ + z) * NY + y) * TOK
                to = seq_of(x, y, z) * TOK
                out[to:to + TOK, :] = total[begin:begin + TOK]


def place(own, received):
    return pl.pallas_call(
        place_kernel,
        in_specs=[pl.BlockSpec(memory_space=pltpu.VMEM)] * 4,
        out_specs=pl.BlockSpec(memory_space=pltpu.VMEM),
        out_shape=jax.ShapeDtypeStruct(own.shape, BF16),
        compiler_params=pltpu.CompilerParams(vmem_limit_bytes=32 * MIB),
    )(own, *received)


def per_device(
    queries, new_keys, new_values, cache_keys, cache_values, cache_lengths, positions, out_weight
):
    y = lax.axis_index("seq") // NZ % NY
    head = lax.axis_index("head")

    length = cache_lengths[0]
    used = jnp.arange(SLOTS, dtype=jnp.int32)[:, None] < length
    keys = jnp.where(used, cache_keys, cache_keys[0:1])
    values = jnp.where(used, cache_values, jnp.zeros((), BF16))
    high, low = (positions // 32).astype(BF16), (positions % 32).astype(BF16)
    meta = jnp.concatenate([
        high[:, None], low[:, None],
        jnp.full((TOK, 1), (length // 64).astype(BF16)),
        jnp.full((TOK, 1), (length % 64).astype(BF16)),
        jnp.zeros((TOK, 2 * HD - 4), BF16)], axis=1)
    block = jnp.concatenate([
        jnp.concatenate([keys, values], axis=1),
        jnp.concatenate([new_keys, new_values], axis=1), meta], axis=0)
    asking = jnp.concatenate(
        [queries, high[:, None], low[:, None], jnp.zeros((TOK, HD - 2), BF16)], axis=1)

    asked = swap(jnp.broadcast_to(asking, (NY * NZ,) + asking.shape), PLANES_YZ)
    asked = asked.reshape(GROUP, asking.shape[1])
    before, after = shift(block, dx=1), shift(block, dx=-1)
    block, asking = lax.optimization_barrier((block, asking))
    asked = swap(jnp.broadcast_to(asking, (NY * NZ,) + asking.shape), PLANES_YZ)
    asked = asked.reshape(GROUP, asking.shape[1])
    across = (shift(before[:CUT], dx=1), shift(after[CUT:], dx=-1))

    other_rows = lax.dynamic_slice_in_dim(out_weight, (1 - y) * HALF, HALF)
    other_rows, asked = lax.optimization_barrier((other_rows, asked))
    theirs = shift(other_rows, dy=1)

    state = attend(asked, [block, before, after], ((0, SLOTS, None),) * 3)
    partial = attend(
        asked, across, ((0, CUT, 3), (CUT, SLOTS - CUT, 3)), state,
        (block, before, after, across[1]))
    merged = merge(swap(partial, PLANES_YZ))
    rows = swap(merged, PLANES_XZ).reshape(-1, HALF)

    kept, sent = project(jnp.stack([y, head // 2, head % 2]).astype(jnp.int32), rows, out_weight, theirs)
    to_core = lax.ppermute(sent, "head", [(h, h ^ 1) for h in range(4)])
    terms = kept + to_core.astype(F32)

    def across_y(value, dy, dlow):
        perm = [
            ((s * 4 + h), (s ^ (dy * NZ)) * 4 + (h ^ (dlow * 2)))
            for s in range(NX * NY * NZ) for h in range(4)]
        return lax.ppermute(value, ("seq", "head"), perm)

    others = [
        across_y(terms[:, k * HD:(k + 1) * HD].astype(BF16), k // 2, k % 2) for k in range(1, 4)]
    return place(terms[:, :HD], others)


def solution(mesh):
    return jax.shard_map(
        per_device,
        mesh=mesh,
        in_specs=(
            P("seq", "head"),
            P("seq", "head"),
            P("seq", "head"),
            P("seq", "head"),
            P("seq", "head"),
            P("seq"),
            P("seq"),
            P("head", "seq"),
        ),
        out_specs=P(None, ("seq", "head")),
        check_vma=False,
    )
```

```python
import functools
import math

import jax
import jax.numpy as jnp
from jax import lax
from jax.experimental import pallas as pl
from jax.experimental.pallas import tpu as pltpu
from jax.sharding import PartitionSpec as P

HD = 128
NX, NY, NZ = 4, 2, 4
SLOTS = 2048
TOK = 32
HEADS = 16
HALF = (HEADS // NY) * HD
PAY = HALF + HD
GROUP = NY * NZ * TOK
PAIRS = HEADS // 2
LANES = 2 * GROUP
DEPTH = HD + 16
NEW0 = SLOTS
META0 = SLOTS + TOK
CUT = 1024
CHUNK = 512
HEADROOM = 60.0
TEMPER = math.log2(math.e) / math.sqrt(HD)
MIB = 2**20
BF16, F32 = jnp.bfloat16, jnp.float32


def seq_of(x, y, z):
    return ((x % NX) * NY + y % NY) * NZ + z % NZ


PLANES_YZ = [[seq_of(x, y, z) for y in range(NY) for z in range(NZ)] for x in range(NX)]
LINES_Z = [[seq_of(x, y, z) for z in range(NZ)] for x in range(NX) for y in range(NY)]


def swap(value, groups):
    return lax.all_to_all(value, "seq", 0, 0, axis_index_groups=groups, tiled=True)


def shift(value, dx=0, dy=0, dz=0):
    perm = [
        (seq_of(x, y, z), seq_of(x + dx, y + dy, z + dz))
        for x in range(NX)
        for y in range(NY)
        for z in range(NZ)
    ]
    return lax.ppermute(value, "seq", perm)


def attend_kernel(first, last, spans, q_ref, *rest):
    rest = list(rest)
    take = lambda n: [rest.pop(0) for _ in range(n)]
    asked_ref = take(1)[0] if last else None
    fresh_refs = take(4) if last else []
    refs = take(len(spans))
    top_in, acc_in = (None, None) if first else take(2)
    out_refs = take(1) if last else take(2)
    top_ref, acc_ref = take(2) if last else out_refs
    high_ref = take(1)[0]

    def length_of(ref, base):
        meta = ref[META0 - base:META0 - base + 16, :].astype(F32)
        return (jnp.max(meta[:, 2:3]) * 64.0 + jnp.max(meta[:, 3:4])).astype(jnp.int32)

    def queries(pair):
        return jnp.concatenate(
            [q_ref[:, (2 * pair + j) * HD:(2 * pair + j + 1) * HD] for j in range(2)], axis=0)

    def score(keys, pair):
        return lax.dot_general(
            keys, queries(pair), (((1,), (1,)), ((), ())), preferred_element_type=F32)

    def chunk_of(ref, base, length, i):
        at = pl.multiple_of(i * CHUNK - base, CHUNK)
        block = ref[pl.ds(at, CHUNK), :]
        slot = lax.broadcasted_iota(jnp.int32, (DEPTH - HD, CHUNK), 1) + i * CHUNK
        ones = jnp.where(slot < length, 1.0, 0.0).astype(BF16)
        return block[:, :HD], jnp.concatenate([block[:, HD:].T, ones], axis=0)

    def eights(s):
        return jnp.max(s.reshape(s.shape[0] // 8, 8, LANES), axis=0)

    if last:
        news = [ref[NEW0 - base:NEW0 - base + TOK, :] for ref, base in zip(fresh_refs, (0, 0, 0, CUT))]
        news = jnp.concatenate(news, axis=0)
        new_keys = news[:, :HD]
        new_values = jnp.concatenate(
            [news[:, HD:].T, jnp.ones((DEPTH - HD, NX * TOK), BF16)], axis=0)
        metas = [ref[META0 - base:META0 - base + TOK, :] for ref, base in zip(fresh_refs, (0, 0, 0, CUT))]
        metas = jnp.concatenate(metas, axis=0).astype(F32)
        given = metas[:, 0:1] * 32.0 + metas[:, 1:2]
        asked = asked_ref[...].astype(F32).T
        asked = asked[0:1] * 32.0 + asked[1:2]
        visible = given <= asked
        visible = jnp.concatenate([visible, visible], axis=1)

    lengths = [length_of(ref, base) for ref, base in spans_of(spans, refs, fresh_refs)]

    def loops(body):
        for ref, (base, slots, _), length in zip(refs, spans, lengths):
            begin, end = base // CHUNK, (base + slots) // CHUNK
            stop = jnp.minimum((length + CHUNK - 1) // CHUNK, end)

            def once(i, _, ref=ref, base=base, length=length):
                body(*chunk_of(ref, base, length, i))
                return 0

            lax.fori_loop(begin, stop, once, 0)

    for pair in range(PAIRS):
        if first:
            top_ref[pair] = jnp.max(score(refs[0][0:CHUNK, :HD], pair), axis=0, keepdims=True)
            acc_ref[pair] = jnp.zeros((DEPTH, LANES), F32)
        else:
            top_ref[pair] = top_in[pair]
            acc_ref[pair] = acc_in[pair]
        high_ref[pair] = jnp.full((8, LANES), -1e30, F32)

    def add(keys, values):
        scores = [score(keys, pair) for pair in range(PAIRS)]
        for pair, s in enumerate(scores):
            high_ref[pair] = jnp.maximum(high_ref[pair], eights(s))
            p = jnp.exp2((s - top_ref[pair]) * TEMPER).astype(BF16)
            acc_ref[pair] += jnp.dot(values, p, preferred_element_type=F32)

    loops(add)
    if last:
        for pair in range(PAIRS):
            s = score(new_keys, pair)
            high_ref[pair] = jnp.maximum(high_ref[pair], eights(jnp.where(visible, s, -1e30)))
            p = jnp.where(visible, jnp.exp2((s - top_ref[pair]) * TEMPER), 0.0).astype(BF16)
            acc_ref[pair] += jnp.dot(new_values, p, preferred_element_type=F32)
    excess = functools.reduce(
        jnp.maximum, [high_ref[pair] - top_ref[pair] for pair in range(PAIRS)])

    @pl.when(jnp.max(excess) * TEMPER > HEADROOM)
    def _():
        for pair in range(PAIRS):
            top_ref[pair] = jnp.full((1, LANES), -1e30, F32) if first else top_in[pair]
            acc_ref[pair] = jnp.zeros((DEPTH, LANES), F32) if first else acc_in[pair]

        def raised(pair, s, values, seen):
            shown = s if seen is None else jnp.where(seen, s, -1e30)
            new = jnp.maximum(top_ref[pair], jnp.max(shown, axis=0, keepdims=True))
            p = jnp.exp2((s - new) * TEMPER)
            p = (p if seen is None else jnp.where(seen, p, 0.0)).astype(BF16)
            keep = jnp.exp2((top_ref[pair] - new) * TEMPER)
            acc_ref[pair] = acc_ref[pair] * keep + jnp.dot(values, p, preferred_element_type=F32)
            top_ref[pair] = new

        def careful(keys, values):
            for pair in range(PAIRS):
                raised(pair, score(keys, pair), values, None)

        loops(careful)
        if last:
            for pair in range(PAIRS):
                raised(pair, score(new_keys, pair), new_values, visible)

    if last:
        out = out_refs[0]
        for half in range(NY):
            levels = []
            for pair in range(half * PAIRS // 2, (half + 1) * PAIRS // 2):
                total = acc_ref[pair, HD:HD + 1, :]
                level = top_ref[pair] * TEMPER + jnp.log2(total)
                part = acc_ref[pair, :HD, :] / total
                for j in range(2):
                    levels.append(level[:, j * GROUP:(j + 1) * GROUP])
                    block = part[:, j * GROUP:(j + 1) * GROUP].T.astype(BF16)
                    at = (2 * pair + j) * HD - half * HALF
                    for z in range(NZ):
                        for y in range(NY):
                            rows = y * NZ * TOK + z * TOK
                            out[half * NZ + z, y * TOK:(y + 1) * TOK, at:at + HD] = (
                                block[rows:rows + TOK])
            level = jnp.concatenate(levels, axis=0)
            high = level.astype(BF16).astype(F32)
            middle = (level - high).astype(BF16).astype(F32)
            low = level - high - middle
            block = jnp.concatenate(
                [high, middle, low, jnp.zeros((HD - 24, GROUP), F32)], axis=0).T.astype(BF16)
            for z in range(NZ):
                for y in range(NY):
                    rows = y * NZ * TOK + z * TOK
                    out[half * NZ + z, y * TOK:(y + 1) * TOK, HALF:] = block[rows:rows + TOK]


def spans_of(spans, refs, fresh_refs):
    for ref, (base, _, holder) in zip(refs, spans):
        yield (ref, base) if holder is None else (fresh_refs[holder], CUT)


def attend(asked, blocks, spans, state=None, fresh=None):
    first, last = state is None, fresh is not None
    operands = [asked] + ([asked] + list(fresh) if last else []) + list(blocks) + list(state or ())
    whole = lambda array: pl.BlockSpec(array.shape, lambda i: (0,) * array.ndim)
    specs = [pl.BlockSpec((GROUP, HEADS * HD), lambda i: (0, 0))]
    if last:
        specs += [pl.BlockSpec((GROUP, HD), lambda i: (0, HEADS))]
    specs += [whole(operand) for operand in operands[len(specs):]]
    held = [
        jax.ShapeDtypeStruct((PAIRS, 1, LANES), F32),
        jax.ShapeDtypeStruct((PAIRS, DEPTH, LANES), F32)]
    results = [jax.ShapeDtypeStruct((NY * NZ, NY * TOK, PAY), BF16)] if last else held
    scratch = [pltpu.VMEM(h.shape, F32) for h in held] if last else []
    keys = sum(slots for _, slots, _ in spans)
    out = pl.pallas_call(
        functools.partial(attend_kernel, first, last, spans),
        grid=(1,),
        in_specs=specs,
        out_specs=[whole(result) for result in results],
        out_shape=results,
        scratch_shapes=scratch + [pltpu.VMEM((PAIRS, 8, LANES), F32)],
        cost_estimate=pl.CostEstimate(
            flops=4 * HEADS * GROUP * HD * keys, transcendentals=HEADS * GROUP * keys,
            bytes_accessed=4 * MIB),
        compiler_params=pltpu.CompilerParams(vmem_limit_bytes=60 * MIB),
    )(*operands)
    return out[0] if last else out


def merge_kernel(pieces, out):
    count = NY * NZ
    split = [pieces[r, :, HALF:].astype(F32) for r in range(count)]
    levels = [term[:, 0:8] + term[:, 8:16] + term[:, 16:24] for term in split]
    top = functools.reduce(jnp.maximum, levels)
    shares = [jnp.exp2(level - top) for level in levels]
    whole = functools.reduce(jnp.add, shares)
    for j in range(HALF // HD):
        total = jnp.zeros((NY * TOK, HD), F32)
        for r in range(count):
            total += shares[r][:, j:j + 1] * pieces[r, :, j * HD:(j + 1) * HD].astype(F32)
        merged = (total / whole[:, j:j + 1]).astype(BF16)
        for to in range(NZ):
            out[to, :, j * HD:(j + 1) * HD] = merged


def merge(pieces):
    return pl.pallas_call(
        merge_kernel,
        in_specs=[pl.BlockSpec(memory_space=pltpu.VMEM)],
        out_specs=pl.BlockSpec(memory_space=pltpu.VMEM),
        out_shape=jax.ShapeDtypeStruct((NZ, NY * TOK, HALF), BF16),
        compiler_params=pltpu.CompilerParams(vmem_limit_bytes=32 * MIB),
    )(pieces)


def project_kernel(dcore, at_ref, *refs):
    *blocks, mine, theirs, out = refs
    low_y, core = at_ref[1], at_ref[2]
    for k, weight in enumerate((mine, theirs)):
        picked = []
        for dlow in range(2):
            head = lax.rem(low_y + dlow, 2) * 2 + lax.rem(core + dcore, 2)
            picked.append(weight[:, pl.ds(pl.multiple_of(head * HD, HD), HD)])
        picked = jnp.concatenate(picked, axis=1)
        begin = 0
        for rows in blocks:
            count = rows.shape[0]
            terms = jnp.dot(rows[...], picked, preferred_element_type=F32)
            out[begin:begin + count, 2 * k * HD:2 * (k + 1) * HD] = terms.astype(out.dtype)
            begin += count


def project(dcore, at, blocks, weight, theirs, dtype):
    count, width = sum(block.shape[0] for block in blocks), theirs.shape[1]
    return pl.pallas_call(
        functools.partial(project_kernel, dcore),
        grid_spec=pltpu.PrefetchScalarGridSpec(
            num_scalar_prefetch=1,
            grid=(1,),
            in_specs=[pl.BlockSpec(block.shape, lambda i, at: (0, 0)) for block in blocks] + [
                pl.BlockSpec((HALF, width), lambda i, at: (at[0], 0)),
                pl.BlockSpec((HALF, width), lambda i, at: (0, 0)),
            ],
            out_specs=pl.BlockSpec((count, width), lambda i, at: (0, 0)),
        ),
        out_shape=jax.ShapeDtypeStruct((count, width), dtype),
        cost_estimate=pl.CostEstimate(
            flops=2 * count * HALF * width, transcendentals=0, bytes_accessed=4 * MIB),
        compiler_params=pltpu.CompilerParams(vmem_limit_bytes=40 * MIB),
    )(at, *blocks, weight, theirs)


def place_kernel(x_ref, near, near1, near2, near3, far, far1, far2, far3, out):
    pieces = []
    for own, others in ((near, (near1, near2, near3)), (far, (far1, far2, far3))):
        total = own[...]
        for other in others:
            total = total + other[...].astype(F32)
        pieces.append(total.astype(BF16))
    for total, places in zip(pieces, ((0, 1, 3), (2,))):
        for n, dx in enumerate(places):
            x = lax.rem(x_ref[0] + dx, NX)
            for z in range(NZ):
                for y in range(NY):
                    begin = ((n * NZ + z) * NY + y) * TOK
                    to = pl.multiple_of(((x * NY + y) * NZ + z) * TOK, TOK)
                    out[pl.ds(to, TOK), :] = total[begin:begin + TOK]


def place(x, pieces):
    return pl.pallas_call(
        place_kernel,
        in_specs=[pl.BlockSpec(memory_space=pltpu.SMEM)]
        + [pl.BlockSpec(memory_space=pltpu.VMEM)] * 8,
        out_specs=pl.BlockSpec(memory_space=pltpu.VMEM),
        out_shape=jax.ShapeDtypeStruct((NX * GROUP, HD), BF16),
        compiler_params=pltpu.CompilerParams(vmem_limit_bytes=32 * MIB),
    )(x, *pieces)


def per_device(
    queries, new_keys, new_values, cache_keys, cache_values, cache_lengths, positions, out_weight
):
    y = lax.axis_index("seq") // NZ % NY
    head = lax.axis_index("head")

    length = cache_lengths[0]
    used = jnp.arange(SLOTS, dtype=jnp.int32)[:, None] < length
    keys = jnp.where(used, cache_keys, cache_keys[0:1])
    values = jnp.where(used, cache_values, jnp.zeros((), BF16))
    high, low = (positions // 32).astype(BF16), (positions % 32).astype(BF16)
    meta = jnp.concatenate([
        high[:, None], low[:, None],
        jnp.full((TOK, 1), (length // 64).astype(BF16)),
        jnp.full((TOK, 1), (length % 64).astype(BF16)),
        jnp.zeros((TOK, 2 * HD - 4), BF16)], axis=1)
    block = jnp.concatenate([
        jnp.concatenate([keys, values], axis=1),
        jnp.concatenate([new_keys, new_values], axis=1), meta], axis=0)
    asking = jnp.concatenate(
        [queries, high[:, None], low[:, None], jnp.zeros((TOK, HD - 2), BF16)], axis=1)

    asked = swap(jnp.broadcast_to(asking, (NY * NZ,) + asking.shape), PLANES_YZ)
    asked = asked.reshape(GROUP, asking.shape[1])
    before, after = shift(block, dx=1), shift(block, dx=-1)
    block, asking = lax.optimization_barrier((block, asking))
    asked = swap(jnp.broadcast_to(asking, (NY * NZ,) + asking.shape), PLANES_YZ)
    asked = asked.reshape(GROUP, asking.shape[1])
    across = (shift(before[:CUT], dx=1), shift(after[CUT:], dx=-1))

    other_rows = lax.dynamic_slice_in_dim(out_weight, (1 - y) * HALF, HALF)
    other_rows, asked = lax.optimization_barrier((other_rows, asked))
    theirs = shift(other_rows, dy=1)

    state = attend(asked, [block, before, after], ((0, SLOTS, None),) * 3)
    partial = attend(
        asked, across, ((0, CUT, 3), (CUT, SLOTS - CUT, 3)), state,
        (block, before, after, across[1]))
    merged = merge(swap(partial, PLANES_YZ))
    rows = swap(merged, LINES_Z).reshape(GROUP, HALF)
    following, preceding, opposite = shift(rows, dx=-1), shift(rows, dx=1), shift(rows, dx=2)

    at = jnp.stack([y, head // 2, head % 2]).astype(jnp.int32)

    def across_y(value, dy, dlow):
        perm = [
            ((s * 4 + h), (s ^ (dy * NZ)) * 4 + (h ^ (dlow * 2)))
            for s in range(NX * NY * NZ) for h in range(4)]
        return lax.ppermute(value, ("seq", "head"), perm)

    def projected(blocks):
        sent = project(1, at, blocks, out_weight, theirs, BF16)
        from_core = lax.ppermute(sent, "head", [(h, h ^ 1) for h in range(4)])
        terms = project(0, at, blocks, out_weight, theirs, F32) + from_core.astype(F32)
        return terms

    def reduced(terms):
        return [terms[:, :HD]] + [
            across_y(terms[:, k * HD:(k + 1) * HD].astype(BF16), k // 2, k % 2)
            for k in range(1, 4)]

    x = jnp.asarray(lax.axis_index("seq") // (NY * NZ), jnp.int32).reshape(1)
    near = projected([rows, following, preceding])
    near_sums = reduced(near)
    opposite, _ = lax.optimization_barrier((opposite, near))
    return place(x, near_sums + reduced(projected([opposite])))


def solution(mesh):
    return jax.shard_map(
        per_device,
        mesh=mesh,
        in_specs=(
            P("seq", "head"),
            P("seq", "head"),
            P("seq", "head"),
            P("seq", "head"),
            P("seq", "head"),
            P("seq"),
            P("seq"),
            P("head", "seq"),
        ),
        out_specs=P(None, ("seq", "head")),
        check_vma=False,
    )
```

```python
import functools
import math

import jax
import jax.numpy as jnp
from jax import lax
from jax.experimental import pallas as pl
from jax.experimental.pallas import tpu as pltpu
from jax.sharding import PartitionSpec as P

HD = 128
NX, NY, NZ = 4, 2, 4
SLOTS = 2048
TOK = 32
HEADS = 16
HALF = (HEADS // NY) * HD
PAY = HALF + HD
GROUP = NY * NZ * TOK
PAIRS = HEADS // 2
LANES = 2 * GROUP
DEPTH = HD + 16
NEW0 = SLOTS
META0 = SLOTS + TOK
CUT = 1024
CHUNK = 512
HEADROOM = 60.0
CHAINS = 4
STRIP = NY * TOK // CHAINS
TEMPER = math.log2(math.e) / math.sqrt(HD)
MIB = 2**20
BF16, F32 = jnp.bfloat16, jnp.float32


def seq_of(x, y, z):
    return ((x % NX) * NY + y % NY) * NZ + z % NZ


PLANES_YZ = [[seq_of(x, y, z) for y in range(NY) for z in range(NZ)] for x in range(NX)]


def swap(value, groups):
    return lax.all_to_all(value, "seq", 0, 0, axis_index_groups=groups, tiled=True)


def shift(value, dx=0, dy=0, dz=0):
    perm = [
        (seq_of(x, y, z), seq_of(x + dx, y + dy, z + dz))
        for x in range(NX)
        for y in range(NY)
        for z in range(NZ)
    ]
    return lax.ppermute(value, "seq", perm)


def attend_kernel(first, last, spans, q_ref, *rest):
    rest = list(rest)
    take = lambda n: [rest.pop(0) for _ in range(n)]
    asked_ref = take(1)[0] if last else None
    fresh_refs = take(4) if last else []
    refs = take(len(spans))
    top_in, acc_in = (None, None) if first else take(2)
    out_refs = take(1) if last else take(2)
    top_ref, acc_ref = take(2) if last else out_refs
    high_ref = take(1)[0]

    def length_of(ref, row):
        meta = ref[row:row + 16, :].astype(F32)
        return (jnp.max(meta[:, 2:3]) * 64.0 + jnp.max(meta[:, 3:4])).astype(jnp.int32)

    def queries(pair):
        return jnp.concatenate(
            [q_ref[:, (2 * pair + j) * HD:(2 * pair + j + 1) * HD] for j in range(2)], axis=0)

    def score(keys, pair):
        return lax.dot_general(
            keys, queries(pair), (((1,), (1,)), ((), ())), preferred_element_type=F32)

    def chunk_of(ref, base, length, i):
        at = pl.multiple_of(i * CHUNK - base, CHUNK)
        block = ref[pl.ds(at, CHUNK), :]
        slot = lax.broadcasted_iota(jnp.int32, (DEPTH - HD, CHUNK), 1) + i * CHUNK
        ones = jnp.where(slot < length, 1.0, 0.0).astype(BF16)
        return block[:, :HD], jnp.concatenate([block[:, HD:].T, ones], axis=0)

    def eights(s):
        return jnp.max(s.reshape(s.shape[0] // 8, 8, LANES), axis=0)

    if last:
        news = [ref[:TOK, :] for ref in fresh_refs]
        news = jnp.concatenate(news, axis=0)
        new_keys = news[:, :HD]
        new_values = jnp.concatenate(
            [news[:, HD:].T, jnp.ones((DEPTH - HD, NX * TOK), BF16)], axis=0)
        metas = [ref[TOK:, :] for ref in fresh_refs]
        metas = jnp.concatenate(metas, axis=0).astype(F32)
        given = metas[:, 0:1] * 32.0 + metas[:, 1:2]
        asked = asked_ref[...].astype(F32).T
        asked = asked[0:1] * 32.0 + asked[1:2]
        visible = given <= asked
        visible = jnp.concatenate([visible, visible], axis=1)

    lengths = [length_of(ref, row) for ref, row in spans_of(spans, refs, fresh_refs)]

    def loops(body, skip=0):
        for n, (ref, (base, slots, _), length) in enumerate(zip(refs, spans, lengths)):
            begin, end = base // CHUNK + (skip if n == 0 else 0), (base + slots) // CHUNK
            stop = jnp.minimum((length + CHUNK - 1) // CHUNK, end)

            def once(i, _, ref=ref, base=base, length=length):
                body(*chunk_of(ref, base, length, i))
                return 0

            lax.fori_loop(begin, stop, once, 0)

    if first:
        keys, values = chunk_of(refs[0], 0, lengths[0], 0)
        scores = [score(keys, pair) for pair in range(PAIRS)]
        for pair, s in enumerate(scores):
            top = jnp.max(s, axis=0, keepdims=True)
            top_ref[pair] = top
            p = jnp.exp2((s - top) * TEMPER).astype(BF16)
            acc_ref[pair] = jnp.dot(values, p, preferred_element_type=F32)
    else:
        for pair in range(PAIRS):
            top_ref[pair] = top_in[pair]
            acc_ref[pair] = acc_in[pair]
    for pair in range(PAIRS):
        high_ref[pair] = jnp.full((8, LANES), -1e30, F32)

    def add(keys, values):
        scores = [score(keys, pair) for pair in range(PAIRS)]
        for pair, s in enumerate(scores):
            high_ref[pair] = jnp.maximum(high_ref[pair], eights(s))
            p = jnp.exp2((s - top_ref[pair]) * TEMPER).astype(BF16)
            acc_ref[pair] += jnp.dot(values, p, preferred_element_type=F32)

    loops(add, 1 if first else 0)
    if last:
        for pair in range(PAIRS):
            s = score(new_keys, pair)
            high_ref[pair] = jnp.maximum(high_ref[pair], eights(jnp.where(visible, s, -1e30)))
            p = jnp.where(visible, jnp.exp2((s - top_ref[pair]) * TEMPER), 0.0).astype(BF16)
            acc_ref[pair] += jnp.dot(new_values, p, preferred_element_type=F32)
    excess = functools.reduce(
        jnp.maximum, [high_ref[pair] - top_ref[pair] for pair in range(PAIRS)])

    @pl.when(jnp.max(excess) * TEMPER > HEADROOM)
    def _():
        for pair in range(PAIRS):
            top_ref[pair] = jnp.full((1, LANES), -1e30, F32) if first else top_in[pair]
            acc_ref[pair] = jnp.zeros((DEPTH, LANES), F32) if first else acc_in[pair]

        def raised(pair, s, values, seen):
            shown = s if seen is None else jnp.where(seen, s, -1e30)
            new = jnp.maximum(top_ref[pair], jnp.max(shown, axis=0, keepdims=True))
            p = jnp.exp2((s - new) * TEMPER)
            p = (p if seen is None else jnp.where(seen, p, 0.0)).astype(BF16)
            keep = jnp.exp2((top_ref[pair] - new) * TEMPER)
            acc_ref[pair] = acc_ref[pair] * keep + jnp.dot(values, p, preferred_element_type=F32)
            top_ref[pair] = new

        def careful(keys, values):
            for pair in range(PAIRS):
                raised(pair, score(keys, pair), values, None)

        loops(careful)
        if last:
            for pair in range(PAIRS):
                raised(pair, score(new_keys, pair), new_values, visible)

    if last:
        out = out_refs[0]
        for half in range(NY):
            levels = []
            for pair in range(half * PAIRS // 2, (half + 1) * PAIRS // 2):
                total = acc_ref[pair, HD:HD + 1, :]
                level = top_ref[pair] * TEMPER + jnp.log2(total)
                part = (acc_ref[pair, :HD, :] * (1.0 / total)).astype(BF16)
                for j in range(2):
                    levels.append(level[:, j * GROUP:(j + 1) * GROUP])
                    block = part[:, j * GROUP:(j + 1) * GROUP].T
                    at = (2 * pair + j) * HD - half * HALF
                    for z in range(NZ):
                        for y in range(NY):
                            rows = y * NZ * TOK + z * TOK
                            out[half * NZ + z, y * TOK:(y + 1) * TOK, at:at + HD] = (
                                block[rows:rows + TOK])
            level = jnp.concatenate(levels, axis=0)
            high = level.astype(BF16).astype(F32)
            middle = (level - high).astype(BF16).astype(F32)
            low = level - high - middle
            block = jnp.concatenate(
                [high, middle, low, jnp.zeros((HD - 24, GROUP), F32)], axis=0).T.astype(BF16)
            for z in range(NZ):
                for y in range(NY):
                    rows = y * NZ * TOK + z * TOK
                    out[half * NZ + z, y * TOK:(y + 1) * TOK, HALF:] = block[rows:rows + TOK]


def spans_of(spans, refs, fresh_refs):
    for ref, (base, _, holder) in zip(refs, spans):
        yield (ref, META0 - base) if holder is None else (fresh_refs[holder], TOK)


def attend(asked, blocks, spans, state=None, fresh=None):
    first, last = state is None, fresh is not None
    operands = [asked] + ([asked] + list(fresh) if last else []) + list(blocks) + list(state or ())
    whole = lambda array: pl.BlockSpec(array.shape, lambda i: (0,) * array.ndim)
    specs = [pl.BlockSpec((GROUP, HEADS * HD), lambda i: (0, 0))]
    if last:
        specs += [pl.BlockSpec((GROUP, HD), lambda i: (0, HEADS))]
        end = lambda array: array.shape[0] // (2 * TOK) - 1
        specs += [
            pl.BlockSpec((2 * TOK, 2 * HD), functools.partial(lambda n, i: (n, 0), end(array)))
            for array in fresh]
    specs += [whole(operand) for operand in operands[len(specs):]]
    held = [
        jax.ShapeDtypeStruct((PAIRS, 1, LANES), F32),
        jax.ShapeDtypeStruct((PAIRS, DEPTH, LANES), F32)]
    results = [jax.ShapeDtypeStruct((NY * NZ, NY * TOK, PAY), BF16)] if last else held
    scratch = [pltpu.VMEM(h.shape, F32) for h in held] if last else []
    keys = sum(slots for _, slots, _ in spans)
    out = pl.pallas_call(
        functools.partial(attend_kernel, first, last, spans),
        grid=(1,),
        in_specs=specs,
        out_specs=[whole(result) for result in results],
        out_shape=results,
        scratch_shapes=scratch + [pltpu.VMEM((PAIRS, 8, LANES), F32)],
        cost_estimate=pl.CostEstimate(
            flops=4 * HEADS * GROUP * HD * keys, transcendentals=HEADS * GROUP * keys,
            bytes_accessed=4 * MIB),
        compiler_params=pltpu.CompilerParams(vmem_limit_bytes=60 * MIB),
    )(*operands)
    return out[0] if last else out


def merge_kernel(pieces, out):
    count = NY * NZ
    split = [pieces[r, :, HALF:].astype(F32) for r in range(count)]
    levels = [term[:, 0:8] + term[:, 8:16] + term[:, 16:24] for term in split]
    top = functools.reduce(jnp.maximum, levels)
    shares = [jnp.exp2(level - top) for level in levels]
    whole = functools.reduce(jnp.add, shares)
    for j in range(HALF // HD):
        total = jnp.zeros((NY * TOK, HD), F32)
        for r in range(count):
            total += shares[r][:, j:j + 1] * pieces[r, :, j * HD:(j + 1) * HD].astype(F32)
        merged = (total / whole[:, j:j + 1]).astype(BF16)
        out[:, j * HD:(j + 1) * HD] = merged


def merge(pieces):
    return pl.pallas_call(
        merge_kernel,
        in_specs=[pl.BlockSpec(memory_space=pltpu.VMEM)],
        out_specs=pl.BlockSpec(memory_space=pltpu.VMEM),
        out_shape=jax.ShapeDtypeStruct((NY * TOK, HALF), BF16),
        compiler_params=pltpu.CompilerParams(vmem_limit_bytes=32 * MIB),
    )(pieces)


def project_kernel(dcore, at_ref, *refs):
    *blocks, mine, theirs, out, rows = refs
    begin = 0
    for block in blocks:
        rows[begin:begin + block.shape[0], :] = block[...]
        begin += block.shape[0]
    low_y, core = at_ref[1], at_ref[2]
    for k, weight in enumerate((mine, theirs)):
        picked = []
        for dlow in range(2):
            head = lax.rem(low_y + dlow, 2) * 2 + lax.rem(core + dcore, 2)
            picked.append(weight[:, pl.ds(pl.multiple_of(head * HD, HD), HD)])
        terms = jnp.dot(
            rows[...], jnp.concatenate(picked, axis=1), preferred_element_type=F32)
        out[:, 2 * k * HD:2 * (k + 1) * HD] = terms.astype(out.dtype)


def project(dcore, at, blocks, weight, theirs, dtype):
    count, width = sum(block.shape[0] for block in blocks), theirs.shape[1]
    return pl.pallas_call(
        functools.partial(project_kernel, dcore),
        grid_spec=pltpu.PrefetchScalarGridSpec(
            num_scalar_prefetch=1,
            grid=(1,),
            in_specs=[pl.BlockSpec(block.shape, lambda i, at: (0, 0)) for block in blocks] + [
                pl.BlockSpec((HALF, width), lambda i, at: (at[0], 0)),
                pl.BlockSpec((HALF, width), lambda i, at: (0, 0)),
            ],
            out_specs=pl.BlockSpec((count, width), lambda i, at: (0, 0)),
            scratch_shapes=[pltpu.VMEM((count, HALF), BF16)],
        ),
        out_shape=jax.ShapeDtypeStruct((count, width), dtype),
        cost_estimate=pl.CostEstimate(
            flops=2 * count * HALF * width, transcendentals=0, bytes_accessed=4 * MIB),
        compiler_params=pltpu.CompilerParams(vmem_limit_bytes=40 * MIB),
    )(at, *blocks, weight, theirs)


def place_kernel(x_ref, z_ref, own, first, second, third, out):
    total = own[...] + first[...].astype(F32) + second[...].astype(F32) + third[...].astype(F32)
    total = total.astype(BF16)
    for chain in range(CHAINS):
        for a in range(4):
            for b in range(4):
                dx, dz = (a, b) if chain % 2 == 0 else (b, a)
                x, z = lax.rem(x_ref[0] + dx, NX), lax.rem(z_ref[0] + dz, NZ)
                y, within = divmod(chain * STRIP, TOK)
                begin = ((chain * 4 + a) * 4 + b) * STRIP
                to = pl.multiple_of(((x * NY + y) * NZ + z) * TOK + within, STRIP)
                out[pl.ds(to, STRIP), :] = total[begin:begin + STRIP]


def place(x, z, own, received):
    return pl.pallas_call(
        place_kernel,
        in_specs=[pl.BlockSpec(memory_space=pltpu.SMEM)] * 2
        + [pl.BlockSpec(memory_space=pltpu.VMEM)] * 4,
        out_specs=pl.BlockSpec(memory_space=pltpu.VMEM),
        out_shape=jax.ShapeDtypeStruct(own.shape, BF16),
        compiler_params=pltpu.CompilerParams(vmem_limit_bytes=32 * MIB),
    )(x, z, own, *received)


def ring(value, axis):
    ahead, behind = {axis: 1}, {axis: -1}
    before, after = shift(value, **ahead), shift(value, **behind)
    middle = value.shape[0] // 2
    return [value, after, shift(before[:middle], **ahead), shift(after[middle:], **behind), before]


def gather(rows):
    pieces = []
    for chain in range(CHAINS):
        axes = ("dz", "dx") if chain % 2 == 0 else ("dx", "dz")
        line = ring(rows[chain * STRIP:(chain + 1) * STRIP], axes[0])
        pieces += ring(jnp.concatenate(line, axis=0), axes[1])
    return pieces


def per_device(
    queries, new_keys, new_values, cache_keys, cache_values, cache_lengths, positions, out_weight
):
    y = lax.axis_index("seq") // NZ % NY
    head = lax.axis_index("head")

    length = cache_lengths[0]
    used = jnp.arange(SLOTS, dtype=jnp.int32)[:, None] < length
    keys = jnp.where(used, cache_keys, cache_keys[0:1])
    values = jnp.where(used, cache_values, jnp.zeros((), BF16))
    high, low = (positions // 32).astype(BF16), (positions % 32).astype(BF16)
    meta = jnp.concatenate([
        high[:, None], low[:, None],
        jnp.full((TOK, 1), (length // 64).astype(BF16)),
        jnp.full((TOK, 1), (length % 64).astype(BF16)),
        jnp.zeros((TOK, 2 * HD - 4), BF16)], axis=1)
    block = jnp.concatenate([
        jnp.concatenate([keys, values], axis=1),
        jnp.concatenate([new_keys, new_values], axis=1), meta], axis=0)
    asking = jnp.concatenate(
        [queries, high[:, None], low[:, None], jnp.zeros((TOK, HD - 2), BF16)], axis=1)

    asked = swap(jnp.broadcast_to(asking, (NY * NZ,) + asking.shape), PLANES_YZ)
    asked = asked.reshape(GROUP, asking.shape[1])
    before, after = shift(block, dx=1), shift(block, dx=-1)
    block, asking = lax.optimization_barrier((block, asking))
    asked = swap(jnp.broadcast_to(asking, (NY * NZ,) + asking.shape), PLANES_YZ)
    asked = asked.reshape(GROUP, asking.shape[1])
    across = (shift(before[:CUT], dx=1), shift(after[CUT:], dx=-1))

    other_rows = lax.dynamic_slice_in_dim(out_weight, (1 - y) * HALF, HALF)
    other_rows, asked = lax.optimization_barrier((other_rows, asked))
    theirs = shift(other_rows, dy=1)

    state = attend(asked, [block, before, after], ((0, SLOTS, None),) * 3)
    state, theirs = lax.optimization_barrier((state, theirs))
    partial = attend(
        asked, across, ((0, CUT, 3), (CUT, SLOTS - CUT, 3)), state,
        (block, before, after, across[1]))
    pieces = gather(merge(swap(partial, PLANES_YZ)))

    at = jnp.stack([y, head // 2, head % 2]).astype(jnp.int32)
    sent = project(1, at, pieces, out_weight, theirs, BF16)
    from_core = lax.ppermute(sent, "head", [(h, h ^ 1) for h in range(4)])
    terms = project(0, at, pieces, out_weight, theirs, F32) + from_core.astype(F32)

    def across_y(value, dy, dlow):
        perm = [
            ((s * 4 + h), (s ^ (dy * NZ)) * 4 + (h ^ (dlow * 2)))
            for s in range(NX * NY * NZ) for h in range(4)]
        return lax.ppermute(value, ("seq", "head"), perm)

    others = [
        across_y(terms[:, k * HD:(k + 1) * HD].astype(BF16), k // 2, k % 2) for k in range(1, 4)]
    me = lax.axis_index("seq")
    scalar = lambda value: jnp.asarray(value, jnp.int32).reshape(1)
    return place(scalar(me // (NY * NZ)), scalar(me % NZ), terms[:, :HD], others)


def solution(mesh):
    return jax.shard_map(
        per_device,
        mesh=mesh,
        in_specs=(
            P("seq", "head"),
            P("seq", "head"),
            P("seq", "head"),
            P("seq", "head"),
            P("seq", "head"),
            P("seq"),
            P("seq"),
            P("head", "seq"),
        ),
        out_specs=P(None, ("seq", "head")),
        check_vma=False,
    )
```

```python
import functools
import math

import jax
import jax.numpy as jnp
from jax import lax
from jax.experimental import pallas as pl
from jax.experimental.pallas import tpu as pltpu
from jax.sharding import PartitionSpec as P

HD = 128
NX, NY, NZ = 4, 2, 4
SLOTS = 2048
TOK = 32
HEADS = 16
HALF = (HEADS // NY) * HD
PAY = HALF + HD
GROUP = NY * NZ * TOK
PAIRS = HEADS // 2
LANES = 2 * GROUP
DEPTH = HD + 16
NEW0 = SLOTS
META0 = SLOTS + TOK
CHUNK = 512
HEADROOM = 60.0
TEMPER = math.log2(math.e) / math.sqrt(HD)
MIB = 2**20
BF16, F32 = jnp.bfloat16, jnp.float32


def seq_of(x, y, z):
    return ((x % NX) * NY + y % NY) * NZ + z % NZ


PLANES_YZ = [[seq_of(x, y, z) for y in range(NY) for z in range(NZ)] for x in range(NX)]
PLANES_XZ = [[seq_of(x, y, z) for x in range(NX) for z in range(NZ)] for y in range(NY)]


def swap(value, groups):
    return lax.all_to_all(value, "seq", 0, 0, axis_index_groups=groups, tiled=True)


def shift(value, dx=0, dy=0, dz=0):
    perm = [
        (seq_of(x, y, z), seq_of(x + dx, y + dy, z + dz))
        for x in range(NX)
        for y in range(NY)
        for z in range(NZ)
    ]
    return lax.ppermute(value, "seq", perm)


def attend_kernel(first, last, spans, q_ref, *rest):
    rest = list(rest)
    take = lambda n: [rest.pop(0) for _ in range(n)]
    asked_ref = take(1)[0] if last else None
    fresh_refs = take(4) if last else []
    refs = take(len(spans))
    top_in, acc_in = (None, None) if first else take(2)
    out_refs = take(1) if last else take(2)
    top_ref, acc_ref = take(2) if last else out_refs
    high_ref = take(1)[0]

    def length_of(ref, row):
        meta = ref[row:row + 16, :].astype(F32)
        return (jnp.max(meta[:, 2:3]) * 64.0 + jnp.max(meta[:, 3:4])).astype(jnp.int32)

    def queries(pair):
        return jnp.concatenate(
            [q_ref[:, (2 * pair + j) * HD:(2 * pair + j + 1) * HD] for j in range(2)], axis=0)

    def score(keys, pair):
        return lax.dot_general(
            keys, queries(pair), (((1,), (1,)), ((), ())), preferred_element_type=F32)

    def chunk_of(ref, base, length, i):
        at = pl.multiple_of(i * CHUNK - base, CHUNK)
        block = ref[pl.ds(at, CHUNK), :]
        slot = lax.broadcasted_iota(jnp.int32, (DEPTH - HD, CHUNK), 1) + i * CHUNK
        ones = jnp.where(slot < length, 1.0, 0.0).astype(BF16)
        return block[:, :HD], jnp.concatenate([block[:, HD:].T, ones], axis=0)

    def eights(s):
        return jnp.max(s.reshape(s.shape[0] // 8, 8, LANES), axis=0)

    if last:
        news = [ref[:TOK, :] for ref in fresh_refs]
        news = jnp.concatenate(news, axis=0)
        new_keys = news[:, :HD]
        new_values = jnp.concatenate(
            [news[:, HD:].T, jnp.ones((DEPTH - HD, NX * TOK), BF16)], axis=0)
        metas = [ref[TOK:, :] for ref in fresh_refs]
        metas = jnp.concatenate(metas, axis=0).astype(F32)
        given = metas[:, 0:1] * 32.0 + metas[:, 1:2]
        asked = asked_ref[...].astype(F32).T
        asked = asked[0:1] * 32.0 + asked[1:2]
        visible = given <= asked
        visible = jnp.concatenate([visible, visible], axis=1)

    lengths = [
        length_of(ref, META0) if holder is None else length_of(fresh_refs[holder], TOK)
        for ref, (_, _, holder) in zip(refs, spans)]

    def loops(body, skip=0):
        for n, (ref, (base, slots, _), length) in enumerate(zip(refs, spans, lengths)):
            begin, end = base // CHUNK + (skip if n == 0 else 0), (base + slots) // CHUNK
            stop = jnp.minimum((length + CHUNK - 1) // CHUNK, end)

            def once(i, _, ref=ref, base=base, length=length):
                body(*chunk_of(ref, base, length, i))
                return 0

            lax.fori_loop(begin, stop, once, 0)

    if first:
        keys, values = chunk_of(refs[0], 0, lengths[0], 0)
        scores = [score(keys, pair) for pair in range(PAIRS)]
        for pair, s in enumerate(scores):
            top = jnp.max(s, axis=0, keepdims=True)
            top_ref[pair] = top
            p = jnp.exp2((s - top) * TEMPER).astype(BF16)
            acc_ref[pair] = jnp.dot(values, p, preferred_element_type=F32)
    else:
        for pair in range(PAIRS):
            top_ref[pair] = top_in[pair]
            acc_ref[pair] = acc_in[pair]
    for pair in range(PAIRS):
        high_ref[pair] = jnp.full((8, LANES), -1e30, F32)

    def add(keys, values):
        scores = [score(keys, pair) for pair in range(PAIRS)]
        for pair, s in enumerate(scores):
            high_ref[pair] = jnp.maximum(high_ref[pair], eights(s))
            p = jnp.exp2((s - top_ref[pair]) * TEMPER).astype(BF16)
            acc_ref[pair] += jnp.dot(values, p, preferred_element_type=F32)

    loops(add, 1 if first else 0)
    if last:
        for pair in range(PAIRS):
            s = score(new_keys, pair)
            high_ref[pair] = jnp.maximum(high_ref[pair], eights(jnp.where(visible, s, -1e30)))
            p = jnp.where(visible, jnp.exp2((s - top_ref[pair]) * TEMPER), 0.0).astype(BF16)
            acc_ref[pair] += jnp.dot(new_values, p, preferred_element_type=F32)
    excess = functools.reduce(
        jnp.maximum, [high_ref[pair] - top_ref[pair] for pair in range(PAIRS)])

    @pl.when(jnp.max(excess) * TEMPER > HEADROOM)
    def _():
        for pair in range(PAIRS):
            top_ref[pair] = jnp.full((1, LANES), -1e30, F32) if first else top_in[pair]
            acc_ref[pair] = jnp.zeros((DEPTH, LANES), F32) if first else acc_in[pair]

        def raised(pair, s, values, seen):
            shown = s if seen is None else jnp.where(seen, s, -1e30)
            new = jnp.maximum(top_ref[pair], jnp.max(shown, axis=0, keepdims=True))
            p = jnp.exp2((s - new) * TEMPER)
            p = (p if seen is None else jnp.where(seen, p, 0.0)).astype(BF16)
            keep = jnp.exp2((top_ref[pair] - new) * TEMPER)
            acc_ref[pair] = acc_ref[pair] * keep + jnp.dot(values, p, preferred_element_type=F32)
            top_ref[pair] = new

        def careful(keys, values):
            for pair in range(PAIRS):
                raised(pair, score(keys, pair), values, None)

        loops(careful)
        if last:
            for pair in range(PAIRS):
                raised(pair, score(new_keys, pair), new_values, visible)

    if last:
        out = out_refs[0]
        for half in range(NY):
            levels = []
            for pair in range(half * PAIRS // 2, (half + 1) * PAIRS // 2):
                total = acc_ref[pair, HD:HD + 1, :]
                level = top_ref[pair] * TEMPER + jnp.log2(total)
                part = (acc_ref[pair, :HD, :] * (1.0 / total)).astype(BF16)
                for j in range(2):
                    levels.append(level[:, j * GROUP:(j + 1) * GROUP])
                    block = part[:, j * GROUP:(j + 1) * GROUP].T
                    at = (2 * pair + j) * HD - half * HALF
                    for z in range(NZ):
                        for y in range(NY):
                            rows = y * NZ * TOK + z * TOK
                            out[half * NZ + z, y * TOK:(y + 1) * TOK, at:at + HD] = (
                                block[rows:rows + TOK])
            level = jnp.concatenate(levels, axis=0)
            high = level.astype(BF16).astype(F32)
            middle = (level - high).astype(BF16).astype(F32)
            low = level - high - middle
            block = jnp.concatenate(
                [high, middle, low, jnp.zeros((HD - 24, GROUP), F32)], axis=0).T.astype(BF16)
            for z in range(NZ):
                for y in range(NY):
                    rows = y * NZ * TOK + z * TOK
                    out[half * NZ + z, y * TOK:(y + 1) * TOK, HALF:] = block[rows:rows + TOK]


def attend(asked, blocks, spans, state=None, fresh=None):
    first, last = state is None, fresh is not None
    operands = [asked] + ([asked] + list(fresh) if last else []) + list(blocks) + list(state or ())
    whole = lambda array: pl.BlockSpec(array.shape, lambda i: (0,) * array.ndim)
    specs = [pl.BlockSpec((GROUP, HEADS * HD), lambda i: (0, 0))]
    if last:
        specs += [pl.BlockSpec((GROUP, HD), lambda i: (0, HEADS))]
        end = lambda array: array.shape[0] // (2 * TOK) - 1
        specs += [
            pl.BlockSpec((2 * TOK, 2 * HD), functools.partial(lambda n, i: (n, 0), end(array)))
            for array in fresh]
    specs += [whole(operand) for operand in operands[len(specs):]]
    held = [
        jax.ShapeDtypeStruct((PAIRS, 1, LANES), F32),
        jax.ShapeDtypeStruct((PAIRS, DEPTH, LANES), F32)]
    results = [jax.ShapeDtypeStruct((NY * NZ, NY * TOK, PAY), BF16)] if last else held
    scratch = [pltpu.VMEM(h.shape, F32) for h in held] if last else []
    keys = sum(slots for _, slots, _ in spans)
    out = pl.pallas_call(
        functools.partial(attend_kernel, first, last, spans),
        grid=(1,),
        in_specs=specs,
        out_specs=[whole(result) for result in results],
        out_shape=results,
        scratch_shapes=scratch + [pltpu.VMEM((PAIRS, 8, LANES), F32)],
        cost_estimate=pl.CostEstimate(
            flops=4 * HEADS * GROUP * HD * keys, transcendentals=HEADS * GROUP * keys,
            bytes_accessed=4 * MIB),
        compiler_params=pltpu.CompilerParams(vmem_limit_bytes=60 * MIB),
    )(*operands)
    return out[0] if last else out


def merge_kernel(pieces, out):
    count = NY * NZ
    split = [pieces[r, :, HALF:].astype(F32) for r in range(count)]
    levels = [term[:, 0:8] + term[:, 8:16] + term[:, 16:24] for term in split]
    top = functools.reduce(jnp.maximum, levels)
    shares = [jnp.exp2(level - top) for level in levels]
    whole = functools.reduce(jnp.add, shares)
    for j in range(HALF // HD):
        total = jnp.zeros((NY * TOK, HD), F32)
        for r in range(count):
            total += shares[r][:, j:j + 1] * pieces[r, :, j * HD:(j + 1) * HD].astype(F32)
        merged = (total / whole[:, j:j + 1]).astype(BF16)
        for to in range(NX * NZ):
            out[to, :, j * HD:(j + 1) * HD] = merged


def merge(pieces):
    return pl.pallas_call(
        merge_kernel,
        in_specs=[pl.BlockSpec(memory_space=pltpu.VMEM)],
        out_specs=pl.BlockSpec(memory_space=pltpu.VMEM),
        out_shape=jax.ShapeDtypeStruct((NX * NZ, NY * TOK, HALF), BF16),
        compiler_params=pltpu.CompilerParams(vmem_limit_bytes=60 * MIB),
    )(pieces)


def project_kernel(dcore, at_ref, rows, mine, theirs, out):
    low_y, core = at_ref[1], at_ref[2]
    for k, weight in enumerate((mine, theirs)):
        picked = []
        for dlow in range(2):
            head = lax.rem(low_y + dlow, 2) * 2 + lax.rem(core + dcore, 2)
            picked.append(weight[:, pl.ds(pl.multiple_of(head * HD, HD), HD)])
        terms = jnp.dot(
            rows[...], jnp.concatenate(picked, axis=1), preferred_element_type=F32)
        out[:, 2 * k * HD:2 * (k + 1) * HD] = terms.astype(out.dtype)


def project(dcore, at, rows, weight, theirs, dtype):
    count, width = rows.shape[0], theirs.shape[1]
    part = count // 4
    return pl.pallas_call(
        functools.partial(project_kernel, dcore),
        grid_spec=pltpu.PrefetchScalarGridSpec(
            num_scalar_prefetch=1,
            grid=(count // part,),
            in_specs=[
                pl.BlockSpec((part, HALF), lambda i, at: (i, 0)),
                pl.BlockSpec((HALF, width), lambda i, at: (at[0], 0)),
                pl.BlockSpec((HALF, width), lambda i, at: (0, 0)),
            ],
            out_specs=pl.BlockSpec((part, width), lambda i, at: (i, 0)),
        ),
        out_shape=jax.ShapeDtypeStruct((count, width), dtype),
        cost_estimate=pl.CostEstimate(
            flops=2 * count * HALF * width, transcendentals=0, bytes_accessed=4 * MIB),
        compiler_params=pltpu.CompilerParams(vmem_limit_bytes=60 * MIB),
    )(at, rows, weight, theirs)


def place_kernel(own, first, second, third, out):
    total = own[...] + first[...].astype(F32) + second[...].astype(F32) + third[...].astype(F32)
    total = total.astype(BF16)
    for x in range(NX):
        for z in range(NZ):
            for y in range(NY):
                begin = ((x * NZ + z) * NY + y) * TOK
                to = seq_of(x, y, z) * TOK
                out[to:to + TOK, :] = total[begin:begin + TOK]


def place(own, received):
    return pl.pallas_call(
        place_kernel,
        in_specs=[pl.BlockSpec(memory_space=pltpu.VMEM)] * 4,
        out_specs=pl.BlockSpec(memory_space=pltpu.VMEM),
        out_shape=jax.ShapeDtypeStruct(own.shape, BF16),
        compiler_params=pltpu.CompilerParams(vmem_limit_bytes=60 * MIB),
    )(own, *received)


def prepare_kernel(length_ref, queries, keys, values, new_keys, new_values, meta, block, asking):
    used = lax.broadcasted_iota(jnp.int32, (SLOTS, HD), 0) < length_ref[0]
    block[:SLOTS, :HD] = jnp.where(used, keys[...], keys[0:1, :])
    block[:SLOTS, HD:] = jnp.where(used, values[...], jnp.zeros((), BF16))
    block[NEW0:META0, :HD] = new_keys[...]
    block[NEW0:META0, HD:] = new_values[...]
    block[META0:, :] = meta[...]
    for to in range(NY * NZ):
        asking[to, :, :HEADS * HD] = queries[...]
        asking[to, :, HEADS * HD:] = meta[:, :HD]


def prepare(length, *operands):
    return pl.pallas_call(
        prepare_kernel,
        in_specs=[pl.BlockSpec(memory_space=pltpu.SMEM)]
        + [pl.BlockSpec(memory_space=pltpu.VMEM)] * len(operands),
        out_specs=[pl.BlockSpec(memory_space=pltpu.VMEM)] * 2,
        out_shape=[
            jax.ShapeDtypeStruct((META0 + TOK, 2 * HD), BF16),
            jax.ShapeDtypeStruct((NY * NZ, TOK, (HEADS + 1) * HD), BF16)],
        compiler_params=pltpu.CompilerParams(vmem_limit_bytes=60 * MIB),
    )(length, *operands)


def per_device(
    queries, new_keys, new_values, cache_keys, cache_values, cache_lengths, positions, out_weight
):
    y = lax.axis_index("seq") // NZ % NY
    head = lax.axis_index("head")

    length = cache_lengths[0]
    high, low = (positions // 32).astype(BF16), (positions % 32).astype(BF16)
    meta = jnp.concatenate([
        high[:, None], low[:, None],
        jnp.full((TOK, 1), (length // 64).astype(BF16)),
        jnp.full((TOK, 1), (length % 64).astype(BF16)),
        jnp.zeros((TOK, 2 * HD - 4), BF16)], axis=1)
    block, asking = prepare(
        cache_lengths, queries, cache_keys, cache_values, new_keys, new_values, meta)

    before, after = shift(block, dx=1), shift(block, dx=-1)
    asked = swap(asking, PLANES_YZ).reshape(GROUP, (HEADS + 1) * HD)
    late, asked = lax.optimization_barrier((block, asked))
    across = shift(late, dx=2)

    state = attend(asked, [block, before, after], ((0, SLOTS, None),) * 3)
    partial = attend(
        asked, [across], ((0, SLOTS, 3),), state, (block, before, after, across))
    rows = swap(merge(swap(partial, PLANES_YZ)), PLANES_XZ).reshape(-1, HALF)

    other_rows = lax.dynamic_slice_in_dim(out_weight, (1 - y) * HALF, HALF)
    theirs = shift(other_rows, dy=1)
    at = jnp.stack([y, head // 2, head % 2]).astype(jnp.int32)
    sent = project(1, at, rows, out_weight, theirs, BF16)
    from_core = lax.ppermute(sent, "head", [(h, h ^ 1) for h in range(4)])
    terms = project(0, at, rows, out_weight, theirs, F32) + from_core.astype(F32)

    def across_y(value, dy, dlow):
        perm = [
            ((s * 4 + h), (s ^ (dy * NZ)) * 4 + (h ^ (dlow * 2)))
            for s in range(NX * NY * NZ) for h in range(4)]
        return lax.ppermute(value, ("seq", "head"), perm)

    others = [
        across_y(terms[:, k * HD:(k + 1) * HD].astype(BF16), k // 2, k % 2) for k in range(1, 4)]
    return place(terms[:, :HD], others)


def solution(mesh):
    return jax.shard_map(
        per_device,
        mesh=mesh,
        in_specs=(
            P("seq", "head"),
            P("seq", "head"),
            P("seq", "head"),
            P("seq", "head"),
            P("seq", "head"),
            P("seq"),
            P("seq"),
            P("head", "seq"),
        ),
        out_specs=P(None, ("seq", "head")),
        check_vma=False,
    )
```

```python
import functools
import math

import jax
import jax.numpy as jnp
from jax import lax
from jax.experimental import pallas as pl
from jax.experimental.pallas import tpu as pltpu
from jax.sharding import PartitionSpec as P

HD = 128
NX, NY, NZ = 4, 2, 4
SLOTS = 2048
TOK = 32
HEADS = 16
HALF = (HEADS // NY) * HD
PAY = HALF + HD
GROUP = NY * NZ * TOK
PAIRS = HEADS // 2
LANES = 2 * GROUP
DEPTH = HD + 16
CUT = SLOTS // 2
NEW0 = SLOTS
META0 = SLOTS + TOK
CHUNK = 512
PIECE = 128
HEADROOM = 60.0
TEMPER = math.log2(math.e) / math.sqrt(HD)
MIB = 2**20
BF16, F32 = jnp.bfloat16, jnp.float32


def seq_of(x, y, z):
    return ((x % NX) * NY + y % NY) * NZ + z % NZ


PLANES_YZ = [[seq_of(x, y, z) for y in range(NY) for z in range(NZ)] for x in range(NX)]
PLANES_XZ = [[seq_of(x, y, z) for x in range(NX) for z in range(NZ)] for y in range(NY)]


def swap(value, groups):
    return lax.all_to_all(value, "seq", 0, 0, axis_index_groups=groups, tiled=True)


def shift(value, dx=0, dy=0, dz=0):
    perm = [
        (seq_of(x, y, z), seq_of(x + dx, y + dy, z + dz))
        for x in range(NX)
        for y in range(NY)
        for z in range(NZ)
    ]
    return lax.ppermute(value, "seq", perm)


def attend_kernel(first, last, spans, q_ref, *rest):
    rest = list(rest)
    take = lambda n: [rest.pop(0) for _ in range(n)]
    asked_ref = take(1)[0] if last else None
    fresh_refs = take(4) if last else []
    refs = take(len(spans))
    top_in, acc_in = (None, None) if first else take(2)
    out_refs = take(1) if last else take(2)
    top_ref, acc_ref = take(2) if last else out_refs
    high_ref, packed_keys, packed_values = take(3)

    def length_of(ref, row):
        meta = ref[row:row + 16, :].astype(F32)
        return (jnp.max(meta[:, 2:3]) * 64.0 + jnp.max(meta[:, 3:4])).astype(jnp.int32)

    def queries(pair):
        return jnp.concatenate(
            [q_ref[:, (2 * pair + j) * HD:(2 * pair + j + 1) * HD] for j in range(2)], axis=0)

    def score(keys, pair):
        return lax.dot_general(
            keys, queries(pair), (((1,), (1,)), ((), ())), preferred_element_type=F32)

    def chunk(i):
        at = pl.multiple_of(i * CHUNK, CHUNK)
        return packed_keys[pl.ds(at, CHUNK), :], packed_values[:, pl.ds(at, CHUNK)]

    def eights(s):
        return jnp.max(s.reshape(s.shape[0] // 8, 8, LANES), axis=0)

    if last:
        news = [ref[:TOK, :] for ref in fresh_refs]
        news = jnp.concatenate(news, axis=0)
        new_keys = news[:, :HD]
        new_values = jnp.concatenate(
            [news[:, HD:].T, jnp.ones((DEPTH - HD, NX * TOK), BF16)], axis=0)
        metas = [ref[TOK:, :] for ref in fresh_refs]
        metas = jnp.concatenate(metas, axis=0).astype(F32)
        given = metas[:, 0:1] * 32.0 + metas[:, 1:2]
        asked = asked_ref[...].astype(F32).T
        asked = asked[0:1] * 32.0 + asked[1:2]
        visible = given <= asked
        visible = jnp.concatenate([visible, visible], axis=1)

    lengths = [
        length_of(fresh_refs[holder], TOK) if last else length_of(refs[holder], CUT + TOK)
        for _, _, holder in spans]

    count = jnp.int32(0)
    for ref, (begin, slots, _), length in zip(refs, spans, lengths):
        pieces = jnp.clip((length - begin + PIECE - 1) // PIECE, 0, slots // PIECE)

        def pack(i, _, ref=ref, begin=begin, length=length, count=count):
            to = pl.multiple_of((count + i) * PIECE, PIECE)
            piece = ref[pl.ds(pl.multiple_of(i * PIECE, PIECE), PIECE), :]
            packed_keys[pl.ds(to, PIECE), :] = piece[:, :HD]
            packed_values[:HD, pl.ds(to, PIECE)] = piece[:, HD:].T
            slot = lax.broadcasted_iota(jnp.int32, (DEPTH - HD, PIECE), 1) + begin + i * PIECE
            packed_values[HD:, pl.ds(to, PIECE)] = jnp.where(slot < length, 1.0, 0.0).astype(BF16)
            return 0

        lax.fori_loop(0, pieces, pack, 0)
        count = count + pieces
    chunks = (count * PIECE + CHUNK - 1) // CHUNK

    def fill(i, _):
        to = pl.multiple_of(i * PIECE, PIECE)
        packed_keys[pl.ds(to, PIECE), :] = packed_keys[:PIECE, :]
        packed_values[:, pl.ds(to, PIECE)] = jnp.zeros((DEPTH, PIECE), BF16)
        return 0

    lax.fori_loop(count, chunks * (CHUNK // PIECE), fill, 0)

    def loops(body, begin=0):
        def once(i, _):
            body(*chunk(i))
            return 0

        lax.fori_loop(begin, chunks, once, 0)

    if first:
        keys, values = chunk(0)
        scores = [score(keys, pair) for pair in range(PAIRS)]
        for pair, s in enumerate(scores):
            top = jnp.max(s, axis=0, keepdims=True)
            top_ref[pair] = top
            p = jnp.exp2((s - top) * TEMPER).astype(BF16)
            acc_ref[pair] = jnp.dot(values, p, preferred_element_type=F32)
    else:
        for pair in range(PAIRS):
            top_ref[pair] = top_in[pair]
            acc_ref[pair] = acc_in[pair]
    for pair in range(PAIRS):
        high_ref[pair] = jnp.full((8, LANES), -1e30, F32)

    def add(keys, values):
        scores = [score(keys, pair) for pair in range(PAIRS)]
        for pair, s in enumerate(scores):
            high_ref[pair] = jnp.maximum(high_ref[pair], eights(s))
            p = jnp.exp2((s - top_ref[pair]) * TEMPER).astype(BF16)
            acc_ref[pair] += jnp.dot(values, p, preferred_element_type=F32)

    loops(add, 1 if first else 0)
    if last:
        for pair in range(PAIRS):
            s = score(new_keys, pair)
            high_ref[pair] = jnp.maximum(high_ref[pair], eights(jnp.where(visible, s, -1e30)))
            p = jnp.where(visible, jnp.exp2((s - top_ref[pair]) * TEMPER), 0.0).astype(BF16)
            acc_ref[pair] += jnp.dot(new_values, p, preferred_element_type=F32)
    excess = functools.reduce(
        jnp.maximum, [high_ref[pair] - top_ref[pair] for pair in range(PAIRS)])

    @pl.when(jnp.max(excess) * TEMPER > HEADROOM)
    def _():
        for pair in range(PAIRS):
            top_ref[pair] = jnp.full((1, LANES), -1e30, F32) if first else top_in[pair]
            acc_ref[pair] = jnp.zeros((DEPTH, LANES), F32) if first else acc_in[pair]

        def raised(pair, s, values, seen):
            shown = s if seen is None else jnp.where(seen, s, -1e30)
            new = jnp.maximum(top_ref[pair], jnp.max(shown, axis=0, keepdims=True))
            p = jnp.exp2((s - new) * TEMPER)
            p = (p if seen is None else jnp.where(seen, p, 0.0)).astype(BF16)
            keep = jnp.exp2((top_ref[pair] - new) * TEMPER)
            acc_ref[pair] = acc_ref[pair] * keep + jnp.dot(values, p, preferred_element_type=F32)
            top_ref[pair] = new

        def careful(keys, values):
            for pair in range(PAIRS):
                raised(pair, score(keys, pair), values, None)

        loops(careful)
        if last:
            for pair in range(PAIRS):
                raised(pair, score(new_keys, pair), new_values, visible)

    if last:
        out = out_refs[0]
        for half in range(NY):
            levels = []
            for pair in range(half * PAIRS // 2, (half + 1) * PAIRS // 2):
                total = acc_ref[pair, HD:HD + 1, :]
                level = top_ref[pair] * TEMPER + jnp.log2(total)
                part = (acc_ref[pair, :HD, :] * (1.0 / total)).astype(BF16)
                for j in range(2):
                    levels.append(level[:, j * GROUP:(j + 1) * GROUP])
                    block = part[:, j * GROUP:(j + 1) * GROUP].T
                    at = (2 * pair + j) * HD - half * HALF
                    for z in range(NZ):
                        for y in range(NY):
                            rows = y * NZ * TOK + z * TOK
                            out[half * NZ + z, y * TOK:(y + 1) * TOK, at:at + HD] = (
                                block[rows:rows + TOK])
            level = jnp.concatenate(levels, axis=0)
            high = level.astype(BF16).astype(F32)
            middle = (level - high).astype(BF16).astype(F32)
            low = level - high - middle
            block = jnp.concatenate(
                [high, middle, low, jnp.zeros((HD - 24, GROUP), F32)], axis=0).T.astype(BF16)
            for z in range(NZ):
                for y in range(NY):
                    rows = y * NZ * TOK + z * TOK
                    out[half * NZ + z, y * TOK:(y + 1) * TOK, HALF:] = block[rows:rows + TOK]


def attend(asked, blocks, spans, state=None, fresh=None):
    first, last = state is None, fresh is not None
    operands = [asked] + ([asked] + list(fresh) if last else []) + list(blocks) + list(state or ())
    whole = lambda array: pl.BlockSpec(array.shape, lambda i: (0,) * array.ndim)
    specs = [pl.BlockSpec((GROUP, HEADS * HD), lambda i: (0, 0))]
    if last:
        specs += [pl.BlockSpec((GROUP, HD), lambda i: (0, HEADS))]
        end = lambda array: array.shape[0] // (2 * TOK) - 1
        specs += [
            pl.BlockSpec((2 * TOK, 2 * HD), functools.partial(lambda n, i: (n, 0), end(array)))
            for array in fresh]
    specs += [whole(operand) for operand in operands[len(specs):]]
    held = [
        jax.ShapeDtypeStruct((PAIRS, 1, LANES), F32),
        jax.ShapeDtypeStruct((PAIRS, DEPTH, LANES), F32)]
    results = [jax.ShapeDtypeStruct((NY * NZ, NY * TOK, PAY), BF16)] if last else held
    scratch = [pltpu.VMEM(h.shape, F32) for h in held] if last else []
    keys = sum(slots for _, slots, _ in spans)
    out = pl.pallas_call(
        functools.partial(attend_kernel, first, last, spans),
        grid=(1,),
        in_specs=specs,
        out_specs=[whole(result) for result in results],
        out_shape=results,
        scratch_shapes=scratch + [
            pltpu.VMEM((PAIRS, 8, LANES), F32),
            pltpu.VMEM((keys, HD), BF16),
            pltpu.VMEM((DEPTH, keys), BF16)],
        cost_estimate=pl.CostEstimate(
            flops=4 * HEADS * GROUP * HD * keys, transcendentals=HEADS * GROUP * keys,
            bytes_accessed=4 * MIB),
        compiler_params=pltpu.CompilerParams(vmem_limit_bytes=40 * MIB),
    )(*operands)
    return out[0] if last else out


def merge_kernel(pieces, out):
    count = NY * NZ
    split = [pieces[r, :, HALF:].astype(F32) for r in range(count)]
    levels = [term[:, 0:8] + term[:, 8:16] + term[:, 16:24] for term in split]
    top = functools.reduce(jnp.maximum, levels)
    shares = [jnp.exp2(level - top) for level in levels]
    whole = functools.reduce(jnp.add, shares)
    for j in range(HALF // HD):
        total = jnp.zeros((NY * TOK, HD), F32)
        for r in range(count):
            total += shares[r][:, j:j + 1] * pieces[r, :, j * HD:(j + 1) * HD].astype(F32)
        merged = (total / whole[:, j:j + 1]).astype(BF16)
        for to in range(NX * NZ):
            out[to, :, j * HD:(j + 1) * HD] = merged


def merge(pieces):
    return pl.pallas_call(
        merge_kernel,
        in_specs=[pl.BlockSpec(memory_space=pltpu.VMEM)],
        out_specs=pl.BlockSpec(memory_space=pltpu.VMEM),
        out_shape=jax.ShapeDtypeStruct((NX * NZ, NY * TOK, HALF), BF16),
        compiler_params=pltpu.CompilerParams(vmem_limit_bytes=32 * MIB),
    )(pieces)


def project_kernel(at_ref, rows, mine, theirs, kept, sent):
    low_y, core = at_ref[1], at_ref[2]
    for dcore, out in ((0, kept), (1, sent)):
        for k, weight in enumerate((mine, theirs)):
            picked = []
            for dlow in range(2):
                head = lax.rem(low_y + dlow, 2) * 2 + lax.rem(core + dcore, 2)
                picked.append(weight[:, pl.ds(pl.multiple_of(head * HD, HD), HD)])
            terms = jnp.dot(
                rows[...], jnp.concatenate(picked, axis=1), preferred_element_type=F32)
            out[:, 2 * k * HD:2 * (k + 1) * HD] = terms.astype(out.dtype)


def project(at, rows, weight, theirs):
    count, width = rows.shape[0], theirs.shape[1]
    part = count // 4
    return pl.pallas_call(
        project_kernel,
        grid_spec=pltpu.PrefetchScalarGridSpec(
            num_scalar_prefetch=1,
            grid=(count // part,),
            in_specs=[
                pl.BlockSpec((part, HALF), lambda i, at: (i, 0)),
                pl.BlockSpec((HALF, width), lambda i, at: (at[0], 0)),
                pl.BlockSpec((HALF, width), lambda i, at: (0, 0)),
            ],
            out_specs=[pl.BlockSpec((part, width), lambda i, at: (i, 0))] * 2,
        ),
        out_shape=[
            jax.ShapeDtypeStruct((count, width), F32),
            jax.ShapeDtypeStruct((count, width), BF16)],
        compiler_params=pltpu.CompilerParams(vmem_limit_bytes=32 * MIB),
    )(at, rows, weight, theirs)


def place_kernel(own, first, second, third, out):
    total = own[...] + first[...].astype(F32) + second[...].astype(F32) + third[...].astype(F32)
    total = total.astype(BF16)
    for x in range(NX):
        for z in range(NZ):
            for y in range(NY):
                begin = ((x * NZ + z) * NY + y) * TOK
                to = seq_of(x, y, z) * TOK
                out[to:to + TOK, :] = total[begin:begin + TOK]


def place(own, received):
    return pl.pallas_call(
        place_kernel,
        in_specs=[pl.BlockSpec(memory_space=pltpu.VMEM)] * 4,
        out_specs=pl.BlockSpec(memory_space=pltpu.VMEM),
        out_shape=jax.ShapeDtypeStruct(own.shape, BF16),
        compiler_params=pltpu.CompilerParams(vmem_limit_bytes=32 * MIB),
    )(own, *received)


def prepare_kernel(length_ref, queries, keys, values, new_keys, new_values, meta, head, tail, asking):
    for out, begin in ((head, 0), (tail, CUT)):
        used = lax.broadcasted_iota(jnp.int32, (CUT, HD), 0) + begin < length_ref[0]
        span = slice(begin, begin + CUT)
        out[:CUT, :HD] = jnp.where(used, keys[span, :], keys[0:1, :])
        out[:CUT, HD:] = jnp.where(used, values[span, :], jnp.zeros((), BF16))
    tail[CUT:CUT + TOK, :HD] = new_keys[...]
    tail[CUT:CUT + TOK, HD:] = new_values[...]
    tail[CUT + TOK:, :] = meta[...]
    for to in range(NY * NZ):
        asking[to, :, :HEADS * HD] = queries[...]
        asking[to, :, HEADS * HD:] = meta[:, :HD]


def prepare(length, *operands):
    return pl.pallas_call(
        prepare_kernel,
        in_specs=[pl.BlockSpec(memory_space=pltpu.SMEM)]
        + [pl.BlockSpec(memory_space=pltpu.VMEM)] * len(operands),
        out_specs=[pl.BlockSpec(memory_space=pltpu.VMEM)] * 3,
        out_shape=[
            jax.ShapeDtypeStruct((CUT, 2 * HD), BF16),
            jax.ShapeDtypeStruct((CUT + 2 * TOK, 2 * HD), BF16),
            jax.ShapeDtypeStruct((NY * NZ, TOK, (HEADS + 1) * HD), BF16)],
        compiler_params=pltpu.CompilerParams(vmem_limit_bytes=32 * MIB),
    )(length, *operands)


def per_device(
    queries, new_keys, new_values, cache_keys, cache_values, cache_lengths, positions, out_weight
):
    y = lax.axis_index("seq") // NZ % NY
    head = lax.axis_index("head")

    length = cache_lengths[0]
    high, low = (positions // 32).astype(BF16), (positions % 32).astype(BF16)
    meta = jnp.concatenate([
        high[:, None], low[:, None],
        jnp.full((TOK, 1), (length // 64).astype(BF16)),
        jnp.full((TOK, 1), (length % 64).astype(BF16)),
        jnp.zeros((TOK, 2 * HD - 4), BF16)], axis=1)
    own_head, own_tail, asking = prepare(
        cache_lengths, queries, cache_keys, cache_values, new_keys, new_values, meta)

    before_head, after_tail = shift(own_head, dx=1), shift(own_tail, dx=-1)
    before_tail, after_head = shift(own_tail, dx=1), shift(own_head, dx=-1)
    asked = swap(asking, PLANES_YZ).reshape(GROUP, (HEADS + 1) * HD)
    far_head, far_tail = shift(before_head, dx=1), shift(after_tail, dx=-1)

    near = [own_head, own_tail, before_head, before_tail, after_head, after_tail]
    state = attend(
        asked, near, tuple((part * CUT, CUT, 2 * n + 1) for n in range(3) for part in range(2)))
    tails = (own_tail, before_tail, after_tail, far_tail)
    partial = attend(
        asked, [far_head, far_tail], ((0, CUT, 3), (CUT, CUT, 3)), state, tails)
    rows = swap(merge(swap(partial, PLANES_YZ)), PLANES_XZ).reshape(-1, HALF)

    other_rows = lax.dynamic_slice_in_dim(out_weight, (1 - y) * HALF, HALF)
    theirs = shift(other_rows, dy=1)
    at = jnp.stack([y, head // 2, head % 2]).astype(jnp.int32)
    kept, sent = project(at, rows, out_weight, theirs)
    from_core = lax.ppermute(sent, "head", [(h, h ^ 1) for h in range(4)])
    terms = kept + from_core.astype(F32)

    def across_y(value, dy, dlow):
        perm = [
            ((s * 4 + h), (s ^ (dy * NZ)) * 4 + (h ^ (dlow * 2)))
            for s in range(NX * NY * NZ) for h in range(4)]
        return lax.ppermute(value, ("seq", "head"), perm)

    others = [
        across_y(terms[:, k * HD:(k + 1) * HD].astype(BF16), k // 2, k % 2) for k in range(1, 4)]
    return place(terms[:, :HD], others)


def solution(mesh):
    return jax.shard_map(
        per_device,
        mesh=mesh,
        in_specs=(
            P("seq", "head"),
            P("seq", "head"),
            P("seq", "head"),
            P("seq", "head"),
            P("seq", "head"),
            P("seq"),
            P("seq"),
            P("head", "seq"),
        ),
        out_specs=P(None, ("seq", "head")),
        check_vma=False,
    )
```

```python
import functools
import math

import jax
import jax.numpy as jnp
from jax import lax
from jax.experimental import pallas as pl
from jax.experimental.pallas import tpu as pltpu
from jax.sharding import PartitionSpec as P

HD = 128
NX, NY, NZ = 4, 2, 4
SLOTS = 2048
TOK = 32
HEADS = 16
HALF = (HEADS // NY) * HD
PAY = HALF + HD
GROUP = NY * NZ * TOK
PAIRS = HEADS // 2
LANES = 2 * GROUP
DEPTH = HD + 16
CUT = SLOTS // 2
NEW0 = SLOTS
META0 = SLOTS + TOK
CHUNK = 512
PIECE = 128
HEADROOM = 60.0
TEMPER = math.log2(math.e) / math.sqrt(HD)
MIB = 2**20
BF16, F32 = jnp.bfloat16, jnp.float32


def seq_of(x, y, z):
    return ((x % NX) * NY + y % NY) * NZ + z % NZ


PLANES_YZ = [[seq_of(x, y, z) for y in range(NY) for z in range(NZ)] for x in range(NX)]
PLANES_XZ = [[seq_of(x, y, z) for x in range(NX) for z in range(NZ)] for y in range(NY)]


def swap(value, groups):
    return lax.all_to_all(value, "seq", 0, 0, axis_index_groups=groups, tiled=True)


def shift(value, dx=0, dy=0, dz=0):
    perm = [
        (seq_of(x, y, z), seq_of(x + dx, y + dy, z + dz))
        for x in range(NX)
        for y in range(NY)
        for z in range(NZ)
    ]
    return lax.ppermute(value, "seq", perm)


def attend_kernel(first, last, spans, q_ref, *rest):
    rest = list(rest)
    take = lambda n: [rest.pop(0) for _ in range(n)]
    asked_ref = take(1)[0] if last else None
    fresh_refs = take(4) if last else []
    refs = take(len(spans))
    top_in, acc_in = (None, None) if first else take(2)
    out_refs = take(1) if last else take(2)
    top_ref, acc_ref = take(2) if last else out_refs
    high_ref, packed_keys, packed_values = take(3)

    def length_of(ref, row):
        meta = ref[row:row + 16, :].astype(F32)
        return (jnp.max(meta[:, 2:3]) * 64.0 + jnp.max(meta[:, 3:4])).astype(jnp.int32)

    def queries(pair):
        return jnp.concatenate(
            [q_ref[:, (2 * pair + j) * HD:(2 * pair + j + 1) * HD] for j in range(2)], axis=0)

    def score(keys, pair):
        return lax.dot_general(
            keys, queries(pair), (((1,), (1,)), ((), ())), preferred_element_type=F32)

    def chunk(i):
        at = pl.multiple_of(i * CHUNK, CHUNK)
        return packed_keys[pl.ds(at, CHUNK), :], packed_values[:, pl.ds(at, CHUNK)]

    def eights(s):
        return jnp.max(s.reshape(s.shape[0] // 8, 8, LANES), axis=0)

    if last:
        news = [ref[:TOK, :] for ref in fresh_refs]
        news = jnp.concatenate(news, axis=0)
        new_keys = news[:, :HD]
        new_values = jnp.concatenate(
            [news[:, HD:].T, jnp.ones((DEPTH - HD, NX * TOK), BF16)], axis=0)
        metas = [ref[TOK:, :] for ref in fresh_refs]
        metas = jnp.concatenate(metas, axis=0).astype(F32)
        given = metas[:, 0:1] * 32.0 + metas[:, 1:2]
        asked = asked_ref[...].astype(F32).T
        asked = asked[0:1] * 32.0 + asked[1:2]
        visible = given <= asked
        visible = jnp.concatenate([visible, visible], axis=1)

    lengths = [
        length_of(fresh_refs[holder], TOK) if last else length_of(refs[holder], META0)
        for _, _, holder in spans]

    count = jnp.int32(0)
    for ref, (begin, slots, _), length in zip(refs, spans, lengths):
        pieces = jnp.clip((length - begin + PIECE - 1) // PIECE, 0, slots // PIECE)

        def pack(i, _, ref=ref, begin=begin, length=length, count=count):
            to = pl.multiple_of((count + i) * PIECE, PIECE)
            piece = ref[pl.ds(pl.multiple_of(i * PIECE, PIECE), PIECE), :]
            packed_keys[pl.ds(to, PIECE), :] = piece[:, :HD]
            packed_values[:HD, pl.ds(to, PIECE)] = piece[:, HD:].T
            slot = lax.broadcasted_iota(jnp.int32, (DEPTH - HD, PIECE), 1) + begin + i * PIECE
            packed_values[HD:, pl.ds(to, PIECE)] = jnp.where(slot < length, 1.0, 0.0).astype(BF16)
            return 0

        lax.fori_loop(0, pieces, pack, 0)
        count = count + pieces
    chunks = (count * PIECE + CHUNK - 1) // CHUNK

    def fill(i, _):
        to = pl.multiple_of(i * PIECE, PIECE)
        packed_keys[pl.ds(to, PIECE), :] = packed_keys[:PIECE, :]
        packed_values[:, pl.ds(to, PIECE)] = jnp.zeros((DEPTH, PIECE), BF16)
        return 0

    lax.fori_loop(count, chunks * (CHUNK // PIECE), fill, 0)

    def loops(body, begin=0):
        def once(i, _):
            body(*chunk(i))
            return 0

        lax.fori_loop(begin, chunks, once, 0)

    if first:
        keys, values = chunk(0)
        scores = [score(keys, pair) for pair in range(PAIRS)]
        for pair, s in enumerate(scores):
            top = jnp.max(s, axis=0, keepdims=True)
            top_ref[pair] = top
            p = jnp.exp2((s - top) * TEMPER).astype(BF16)
            acc_ref[pair] = jnp.dot(values, p, preferred_element_type=F32)
    else:
        for pair in range(PAIRS):
            top_ref[pair] = top_in[pair]
            acc_ref[pair] = acc_in[pair]
    for pair in range(PAIRS):
        high_ref[pair] = jnp.full((8, LANES), -1e30, F32)

    def add(keys, values):
        scores = [score(keys, pair) for pair in range(PAIRS)]
        for pair, s in enumerate(scores):
            high_ref[pair] = jnp.maximum(high_ref[pair], eights(s))
            p = jnp.exp2((s - top_ref[pair]) * TEMPER).astype(BF16)
            acc_ref[pair] += jnp.dot(values, p, preferred_element_type=F32)

    loops(add, 1 if first else 0)
    if last:
        for pair in range(PAIRS):
            s = score(new_keys, pair)
            high_ref[pair] = jnp.maximum(high_ref[pair], eights(jnp.where(visible, s, -1e30)))
            p = jnp.where(visible, jnp.exp2((s - top_ref[pair]) * TEMPER), 0.0).astype(BF16)
            acc_ref[pair] += jnp.dot(new_values, p, preferred_element_type=F32)
    excess = functools.reduce(
        jnp.maximum, [high_ref[pair] - top_ref[pair] for pair in range(PAIRS)])

    @pl.when(jnp.max(excess) * TEMPER > HEADROOM)
    def _():
        for pair in range(PAIRS):
            top_ref[pair] = jnp.full((1, LANES), -1e30, F32) if first else top_in[pair]
            acc_ref[pair] = jnp.zeros((DEPTH, LANES), F32) if first else acc_in[pair]

        def raised(pair, s, values, seen):
            shown = s if seen is None else jnp.where(seen, s, -1e30)
            new = jnp.maximum(top_ref[pair], jnp.max(shown, axis=0, keepdims=True))
            p = jnp.exp2((s - new) * TEMPER)
            p = (p if seen is None else jnp.where(seen, p, 0.0)).astype(BF16)
            keep = jnp.exp2((top_ref[pair] - new) * TEMPER)
            acc_ref[pair] = acc_ref[pair] * keep + jnp.dot(values, p, preferred_element_type=F32)
            top_ref[pair] = new

        def careful(keys, values):
            for pair in range(PAIRS):
                raised(pair, score(keys, pair), values, None)

        loops(careful)
        if last:
            for pair in range(PAIRS):
                raised(pair, score(new_keys, pair), new_values, visible)

    if last:
        out = out_refs[0]
        for half in range(NY):
            levels = []
            for pair in range(half * PAIRS // 2, (half + 1) * PAIRS // 2):
                total = acc_ref[pair, HD:HD + 1, :]
                level = top_ref[pair] * TEMPER + jnp.log2(total)
                part = (acc_ref[pair, :HD, :] * (1.0 / total)).astype(BF16)
                for j in range(2):
                    levels.append(level[:, j * GROUP:(j + 1) * GROUP])
                    block = part[:, j * GROUP:(j + 1) * GROUP].T
                    at = (2 * pair + j) * HD - half * HALF
                    for z in range(NZ):
                        for y in range(NY):
                            rows = y * NZ * TOK + z * TOK
                            out[half * NZ + z, y * TOK:(y + 1) * TOK, at:at + HD] = (
                                block[rows:rows + TOK])
            level = jnp.concatenate(levels, axis=0)
            high = level.astype(BF16).astype(F32)
            middle = (level - high).astype(BF16).astype(F32)
            low = level - high - middle
            block = jnp.concatenate(
                [high, middle, low, jnp.zeros((HD - 24, GROUP), F32)], axis=0).T.astype(BF16)
            for z in range(NZ):
                for y in range(NY):
                    rows = y * NZ * TOK + z * TOK
                    out[half * NZ + z, y * TOK:(y + 1) * TOK, HALF:] = block[rows:rows + TOK]


def attend(asked, blocks, spans, state=None, fresh=None):
    first, last = state is None, fresh is not None
    operands = [asked] + ([asked] + list(fresh) if last else []) + list(blocks) + list(state or ())
    whole = lambda array: pl.BlockSpec(array.shape, lambda i: (0,) * array.ndim)
    specs = [pl.BlockSpec((GROUP, HEADS * HD), lambda i: (0, 0))]
    if last:
        specs += [pl.BlockSpec((GROUP, HD), lambda i: (0, HEADS))]
        end = lambda array: array.shape[0] // (2 * TOK) - 1
        specs += [
            pl.BlockSpec((2 * TOK, 2 * HD), functools.partial(lambda n, i: (n, 0), end(array)))
            for array in fresh]
    specs += [whole(operand) for operand in operands[len(specs):]]
    held = [
        jax.ShapeDtypeStruct((PAIRS, 1, LANES), F32),
        jax.ShapeDtypeStruct((PAIRS, DEPTH, LANES), F32)]
    results = [jax.ShapeDtypeStruct((NY * NZ, NY * TOK, PAY), BF16)] if last else held
    scratch = [pltpu.VMEM(h.shape, F32) for h in held] if last else []
    keys = sum(slots for _, slots, _ in spans)
    out = pl.pallas_call(
        functools.partial(attend_kernel, first, last, spans),
        grid=(1,),
        in_specs=specs,
        out_specs=[whole(result) for result in results],
        out_shape=results,
        scratch_shapes=scratch + [
            pltpu.VMEM((PAIRS, 8, LANES), F32),
            pltpu.VMEM((keys, HD), BF16),
            pltpu.VMEM((DEPTH, keys), BF16)],
        cost_estimate=pl.CostEstimate(
            flops=4 * HEADS * GROUP * HD * keys, transcendentals=HEADS * GROUP * keys,
            bytes_accessed=4 * MIB),
        compiler_params=pltpu.CompilerParams(vmem_limit_bytes=40 * MIB),
    )(*operands)
    return out[0] if last else out


def merge_kernel(pieces, out):
    count = NY * NZ
    split = [pieces[r, :, HALF:].astype(F32) for r in range(count)]
    levels = [term[:, 0:8] + term[:, 8:16] + term[:, 16:24] for term in split]
    top = functools.reduce(jnp.maximum, levels)
    shares = [jnp.exp2(level - top) for level in levels]
    whole = functools.reduce(jnp.add, shares)
    for j in range(HALF // HD):
        total = jnp.zeros((NY * TOK, HD), F32)
        for r in range(count):
            total += shares[r][:, j:j + 1] * pieces[r, :, j * HD:(j + 1) * HD].astype(F32)
        merged = (total / whole[:, j:j + 1]).astype(BF16)
        for to in range(NX * NZ):
            out[to, :, j * HD:(j + 1) * HD] = merged


def merge(pieces):
    return pl.pallas_call(
        merge_kernel,
        in_specs=[pl.BlockSpec(memory_space=pltpu.VMEM)],
        out_specs=pl.BlockSpec(memory_space=pltpu.VMEM),
        out_shape=jax.ShapeDtypeStruct((NX * NZ, NY * TOK, HALF), BF16),
        compiler_params=pltpu.CompilerParams(vmem_limit_bytes=32 * MIB),
    )(pieces)


def project_kernel(at_ref, rows, mine, theirs, kept, sent):
    low_y, core = at_ref[1], at_ref[2]
    for dcore, out in ((0, kept), (1, sent)):
        for k, weight in enumerate((mine, theirs)):
            picked = []
            for dlow in range(2):
                head = lax.rem(low_y + dlow, 2) * 2 + lax.rem(core + dcore, 2)
                picked.append(weight[:, pl.ds(pl.multiple_of(head * HD, HD), HD)])
            terms = jnp.dot(
                rows[...], jnp.concatenate(picked, axis=1), preferred_element_type=F32)
            out[:, 2 * k * HD:2 * (k + 1) * HD] = terms.astype(out.dtype)


def project(at, rows, weight, theirs):
    count, width = rows.shape[0], theirs.shape[1]
    part = count // 4
    return pl.pallas_call(
        project_kernel,
        grid_spec=pltpu.PrefetchScalarGridSpec(
            num_scalar_prefetch=1,
            grid=(count // part,),
            in_specs=[
                pl.BlockSpec((part, HALF), lambda i, at: (i, 0)),
                pl.BlockSpec((HALF, width), lambda i, at: (at[0], 0)),
                pl.BlockSpec((HALF, width), lambda i, at: (0, 0)),
            ],
            out_specs=[pl.BlockSpec((part, width), lambda i, at: (i, 0))] * 2,
        ),
        out_shape=[
            jax.ShapeDtypeStruct((count, width), F32),
            jax.ShapeDtypeStruct((count, width), BF16)],
        compiler_params=pltpu.CompilerParams(vmem_limit_bytes=32 * MIB),
    )(at, rows, weight, theirs)


def place_kernel(own, first, second, third, out):
    total = own[...] + first[...].astype(F32) + second[...].astype(F32) + third[...].astype(F32)
    total = total.astype(BF16)
    for x in range(NX):
        for z in range(NZ):
            for y in range(NY):
                begin = ((x * NZ + z) * NY + y) * TOK
                to = seq_of(x, y, z) * TOK
                out[to:to + TOK, :] = total[begin:begin + TOK]


def place(own, received):
    return pl.pallas_call(
        place_kernel,
        in_specs=[pl.BlockSpec(memory_space=pltpu.VMEM)] * 4,
        out_specs=pl.BlockSpec(memory_space=pltpu.VMEM),
        out_shape=jax.ShapeDtypeStruct(own.shape, BF16),
        compiler_params=pltpu.CompilerParams(vmem_limit_bytes=32 * MIB),
    )(own, *received)


def prepare_kernel(length_ref, keys, values, new_keys, new_values, meta, block):
    used = lax.broadcasted_iota(jnp.int32, (SLOTS, HD), 0) < length_ref[0]
    block[:SLOTS, :HD] = jnp.where(used, keys[...], keys[0:1, :])
    block[:SLOTS, HD:] = jnp.where(used, values[...], jnp.zeros((), BF16))
    block[SLOTS:SLOTS + TOK, :HD] = new_keys[...]
    block[SLOTS:SLOTS + TOK, HD:] = new_values[...]
    block[SLOTS + TOK:, :] = meta[...]


def prepare(length, *operands):
    return pl.pallas_call(
        prepare_kernel,
        in_specs=[pl.BlockSpec(memory_space=pltpu.SMEM)]
        + [pl.BlockSpec(memory_space=pltpu.VMEM)] * len(operands),
        out_specs=pl.BlockSpec(memory_space=pltpu.VMEM),
        out_shape=jax.ShapeDtypeStruct((SLOTS + 2 * TOK, 2 * HD), BF16),
        compiler_params=pltpu.CompilerParams(vmem_limit_bytes=60 * MIB),
    )(length, *operands)


def per_device(
    queries, new_keys, new_values, cache_keys, cache_values, cache_lengths, positions, out_weight
):
    y = lax.axis_index("seq") // NZ % NY
    head = lax.axis_index("head")

    length = cache_lengths[0]
    high, low = (positions // 32).astype(BF16), (positions % 32).astype(BF16)
    meta = jnp.concatenate([
        high[:, None], low[:, None],
        jnp.full((TOK, 1), (length // 64).astype(BF16)),
        jnp.full((TOK, 1), (length % 64).astype(BF16)),
        jnp.zeros((TOK, 2 * HD - 4), BF16)], axis=1)
    block = prepare(cache_lengths, cache_keys, cache_values, new_keys, new_values, meta)

    before, after = shift(block, dx=1), shift(block, dx=-1)
    block, queries, meta = lax.optimization_barrier((block, queries, meta))
    asking = jnp.concatenate([queries, meta[:, :HD]], axis=1)
    asking = jnp.broadcast_to(asking, (NY * NZ,) + asking.shape)
    asked = swap(asking, PLANES_YZ).reshape(GROUP, (HEADS + 1) * HD)
    far_head, far_tail = shift(before[:CUT], dx=1), shift(after[CUT:], dx=-1)

    near = [block, before, after]
    state = attend(asked, near, tuple((0, SLOTS, n) for n in range(3)))
    partial = attend(
        asked, [far_head, far_tail], ((0, CUT, 3), (CUT, CUT, 3)), state, near + [far_tail])
    rows = swap(merge(swap(partial, PLANES_YZ)), PLANES_XZ).reshape(-1, HALF)

    other_rows = lax.dynamic_slice_in_dim(out_weight, (1 - y) * HALF, HALF)
    theirs = shift(other_rows, dy=1)
    at = jnp.stack([y, head // 2, head % 2]).astype(jnp.int32)
    kept, sent = project(at, rows, out_weight, theirs)
    from_core = lax.ppermute(sent, "head", [(h, h ^ 1) for h in range(4)])
    terms = kept + from_core.astype(F32)

    def across_y(value, dy, dlow):
        perm = [
            ((s * 4 + h), (s ^ (dy * NZ)) * 4 + (h ^ (dlow * 2)))
            for s in range(NX * NY * NZ) for h in range(4)]
        return lax.ppermute(value, ("seq", "head"), perm)

    others = [
        across_y(terms[:, k * HD:(k + 1) * HD].astype(BF16), k // 2, k % 2) for k in range(1, 4)]
    return place(terms[:, :HD], others)


def solution(mesh):
    return jax.shard_map(
        per_device,
        mesh=mesh,
        in_specs=(
            P("seq", "head"),
            P("seq", "head"),
            P("seq", "head"),
            P("seq", "head"),
            P("seq", "head"),
            P("seq"),
            P("seq"),
            P("head", "seq"),
        ),
        out_specs=P(None, ("seq", "head")),
        check_vma=False,
    )
```

```python
import functools
import math

import jax
import jax.numpy as jnp
from jax import lax
from jax.experimental import pallas as pl
from jax.experimental.pallas import tpu as pltpu
from jax.sharding import PartitionSpec as P

HD = 128
NX, NY, NZ = 4, 2, 4
SLOTS = 2048
TOK = 32
HEADS = 16
HALF = (HEADS // NY) * HD
PAY = HALF + HD
GROUP = NY * NZ * TOK
PAIRS = HEADS // 2
LANES = 2 * GROUP
DEPTH = HD + 16
CUT = SLOTS // 2
NEW0 = SLOTS
META0 = SLOTS + TOK
CHUNK = 512
PIECE = 128
HEADROOM = 2.0**60
TEMPER = math.log2(math.e) / math.sqrt(HD)
MIB = 2**20
BF16, F32 = jnp.bfloat16, jnp.float32


def seq_of(x, y, z):
    return ((x % NX) * NY + y % NY) * NZ + z % NZ


PLANES_YZ = [[seq_of(x, y, z) for y in range(NY) for z in range(NZ)] for x in range(NX)]
PLANES_XZ = [[seq_of(x, y, z) for x in range(NX) for z in range(NZ)] for y in range(NY)]


def swap(value, groups):
    return lax.all_to_all(value, "seq", 0, 0, axis_index_groups=groups, tiled=True)


def shift(value, dx=0, dy=0, dz=0):
    perm = [
        (seq_of(x, y, z), seq_of(x + dx, y + dy, z + dz))
        for x in range(NX)
        for y in range(NY)
        for z in range(NZ)
    ]
    return lax.ppermute(value, "seq", perm)


def attend_kernel(first, last, spans, q_ref, *rest):
    rest = list(rest)
    take = lambda n: [rest.pop(0) for _ in range(n)]
    asked_ref = take(1)[0] if last else None
    fresh_refs = take(4) if last else []
    refs = take(len(spans))
    top_in, acc_in = (None, None) if first else take(2)
    out_refs = take(1) if last else take(2)
    top_ref, acc_ref = take(2) if last else out_refs
    packed_keys, packed_values = take(2)

    def length_of(ref, row):
        meta = ref[row:row + 16, :].astype(F32)
        return (jnp.max(meta[:, 2:3]) * 64.0 + jnp.max(meta[:, 3:4])).astype(jnp.int32)

    def queries(pair):
        return jnp.concatenate(
            [q_ref[:, (2 * pair + j) * HD:(2 * pair + j + 1) * HD] for j in range(2)], axis=0)

    def score(keys, pair):
        return lax.dot_general(
            keys, queries(pair), (((1,), (1,)), ((), ())), preferred_element_type=F32)

    def chunk(i):
        at = pl.multiple_of(i * CHUNK, CHUNK)
        return packed_keys[pl.ds(at, CHUNK), :], packed_values[:, pl.ds(at, CHUNK)]

    if last:
        news = [ref[:TOK, :] for ref in fresh_refs]
        news = jnp.concatenate(news, axis=0)
        new_keys = news[:, :HD]
        new_values = jnp.concatenate(
            [news[:, HD:].T, jnp.ones((DEPTH - HD, NX * TOK), BF16)], axis=0)
        metas = [ref[TOK:, :] for ref in fresh_refs]
        metas = jnp.concatenate(metas, axis=0).astype(F32)
        given = metas[:, 0:1] * 32.0 + metas[:, 1:2]
        asked = asked_ref[...].astype(F32).T
        asked = asked[0:1] * 32.0 + asked[1:2]
        visible = given <= asked
        visible = jnp.concatenate([visible, visible], axis=1)

    lengths = [
        length_of(fresh_refs[holder], TOK) if last else length_of(refs[holder], META0)
        for _, _, holder in spans]

    count = jnp.int32(0)
    for ref, (begin, slots, _), length in zip(refs, spans, lengths):
        pieces = jnp.clip((length - begin + PIECE - 1) // PIECE, 0, slots // PIECE)

        def pack(i, _, ref=ref, begin=begin, length=length, count=count):
            to = pl.multiple_of((count + i) * PIECE, PIECE)
            piece = ref[pl.ds(pl.multiple_of(i * PIECE, PIECE), PIECE), :]
            packed_keys[pl.ds(to, PIECE), :] = piece[:, :HD]
            packed_values[:HD, pl.ds(to, PIECE)] = piece[:, HD:].T
            slot = lax.broadcasted_iota(jnp.int32, (DEPTH - HD, PIECE), 1) + begin + i * PIECE
            packed_values[HD:, pl.ds(to, PIECE)] = jnp.where(slot < length, 1.0, 0.0).astype(BF16)
            return 0

        lax.fori_loop(0, pieces, pack, 0)
        count = count + pieces
    chunks = (count * PIECE + CHUNK - 1) // CHUNK

    def fill(i, _):
        to = pl.multiple_of(i * PIECE, PIECE)
        packed_keys[pl.ds(to, PIECE), :] = packed_keys[:PIECE, :]
        packed_values[:, pl.ds(to, PIECE)] = jnp.zeros((DEPTH, PIECE), BF16)
        return 0

    lax.fori_loop(count, chunks * (CHUNK // PIECE), fill, 0)

    def loops(body, begin=0):
        def once(i, _):
            body(*chunk(i))
            return 0

        lax.fori_loop(begin, chunks, once, 0)

    if first:
        keys, values = chunk(0)
        scores = [score(keys, pair) for pair in range(PAIRS)]
        for pair, s in enumerate(scores):
            top = jnp.max(s, axis=0, keepdims=True)
            top_ref[pair] = top
            p = jnp.exp2((s - top) * TEMPER).astype(BF16)
            acc_ref[pair] = jnp.dot(values, p, preferred_element_type=F32)
    else:
        for pair in range(PAIRS):
            top_ref[pair] = top_in[pair]
            acc_ref[pair] = acc_in[pair]

    def add(keys, values):
        scores = [score(keys, pair) for pair in range(PAIRS)]
        for pair, s in enumerate(scores):
            p = jnp.exp2((s - top_ref[pair]) * TEMPER).astype(BF16)
            acc_ref[pair] += jnp.dot(values, p, preferred_element_type=F32)

    loops(add, 1 if first else 0)
    if last:
        for pair in range(PAIRS):
            s = score(new_keys, pair)
            p = jnp.where(visible, jnp.exp2((s - top_ref[pair]) * TEMPER), 0.0).astype(BF16)
            acc_ref[pair] += jnp.dot(new_values, p, preferred_element_type=F32)
    totals = jnp.concatenate([acc_ref[pair, HD:HD + 1, :] for pair in range(PAIRS)], axis=0)
    wild = jnp.where(totals < HEADROOM, 0.0, 1.0)

    @pl.when(jnp.max(wild) > 0.0)
    def _():
        for pair in range(PAIRS):
            top_ref[pair] = jnp.full((1, LANES), -1e30, F32) if first else top_in[pair]
            acc_ref[pair] = jnp.zeros((DEPTH, LANES), F32) if first else acc_in[pair]

        def raised(pair, s, values, seen):
            shown = s if seen is None else jnp.where(seen, s, -1e30)
            new = jnp.maximum(top_ref[pair], jnp.max(shown, axis=0, keepdims=True))
            p = jnp.exp2((s - new) * TEMPER)
            p = (p if seen is None else jnp.where(seen, p, 0.0)).astype(BF16)
            keep = jnp.exp2((top_ref[pair] - new) * TEMPER)
            acc_ref[pair] = acc_ref[pair] * keep + jnp.dot(values, p, preferred_element_type=F32)
            top_ref[pair] = new

        def careful(keys, values):
            for pair in range(PAIRS):
                raised(pair, score(keys, pair), values, None)

        loops(careful)
        if last:
            for pair in range(PAIRS):
                raised(pair, score(new_keys, pair), new_values, visible)

    if last:
        out = out_refs[0]
        for half in range(NY):
            levels = []
            for pair in range(half * PAIRS // 2, (half + 1) * PAIRS // 2):
                total = acc_ref[pair, HD:HD + 1, :]
                level = top_ref[pair] * TEMPER + jnp.log2(total)
                part = (acc_ref[pair, :HD, :] * (1.0 / total)).astype(BF16)
                for j in range(2):
                    levels.append(level[:, j * GROUP:(j + 1) * GROUP])
                    block = part[:, j * GROUP:(j + 1) * GROUP].T
                    at = (2 * pair + j) * HD - half * HALF
                    for z in range(NZ):
                        for y in range(NY):
                            rows = y * NZ * TOK + z * TOK
                            out[half * NZ + z, y * TOK:(y + 1) * TOK, at:at + HD] = (
                                block[rows:rows + TOK])
            level = jnp.concatenate(levels, axis=0)
            high = level.astype(BF16).astype(F32)
            middle = (level - high).astype(BF16).astype(F32)
            low = level - high - middle
            block = jnp.concatenate(
                [high, middle, low, jnp.zeros((HD - 24, GROUP), F32)], axis=0).T.astype(BF16)
            for z in range(NZ):
                for y in range(NY):
                    rows = y * NZ * TOK + z * TOK
                    out[half * NZ + z, y * TOK:(y + 1) * TOK, HALF:] = block[rows:rows + TOK]


def attend(asked, blocks, spans, state=None, fresh=None):
    first, last = state is None, fresh is not None
    operands = [asked] + ([asked] + list(fresh) if last else []) + list(blocks) + list(state or ())
    whole = lambda array: pl.BlockSpec(array.shape, lambda i: (0,) * array.ndim)
    specs = [pl.BlockSpec((GROUP, HEADS * HD), lambda i: (0, 0))]
    if last:
        specs += [pl.BlockSpec((GROUP, HD), lambda i: (0, HEADS))]
        end = lambda array: array.shape[0] // (2 * TOK) - 1
        specs += [
            pl.BlockSpec((2 * TOK, 2 * HD), functools.partial(lambda n, i: (n, 0), end(array)))
            for array in fresh]
    specs += [whole(operand) for operand in operands[len(specs):]]
    held = [
        jax.ShapeDtypeStruct((PAIRS, 1, LANES), F32),
        jax.ShapeDtypeStruct((PAIRS, DEPTH, LANES), F32)]
    results = [jax.ShapeDtypeStruct((NY * NZ, NY * TOK, PAY), BF16)] if last else held
    scratch = [pltpu.VMEM(h.shape, F32) for h in held] if last else []
    keys = sum(slots for _, slots, _ in spans)
    out = pl.pallas_call(
        functools.partial(attend_kernel, first, last, spans),
        grid=(1,),
        in_specs=specs,
        out_specs=[whole(result) for result in results],
        out_shape=results,
        scratch_shapes=scratch + [
            pltpu.VMEM((keys, HD), BF16),
            pltpu.VMEM((DEPTH, keys), BF16)],
        cost_estimate=pl.CostEstimate(
            flops=4 * HEADS * GROUP * HD * keys, transcendentals=HEADS * GROUP * keys,
            bytes_accessed=4 * MIB),
        compiler_params=pltpu.CompilerParams(vmem_limit_bytes=40 * MIB),
    )(*operands)
    return out[0] if last else out


def merge_kernel(pieces, out):
    count = NY * NZ
    split = [pieces[r, :, HALF:].astype(F32) for r in range(count)]
    levels = [term[:, 0:8] + term[:, 8:16] + term[:, 16:24] for term in split]
    top = functools.reduce(jnp.maximum, levels)
    shares = [jnp.exp2(level - top) for level in levels]
    whole = functools.reduce(jnp.add, shares)
    for j in range(HALF // HD):
        total = jnp.zeros((NY * TOK, HD), F32)
        for r in range(count):
            total += shares[r][:, j:j + 1] * pieces[r, :, j * HD:(j + 1) * HD].astype(F32)
        merged = (total / whole[:, j:j + 1]).astype(BF16)
        for to in range(NX * NZ):
            out[to, :, j * HD:(j + 1) * HD] = merged


def merge(pieces):
    return pl.pallas_call(
        merge_kernel,
        in_specs=[pl.BlockSpec(memory_space=pltpu.VMEM)],
        out_specs=pl.BlockSpec(memory_space=pltpu.VMEM),
        out_shape=jax.ShapeDtypeStruct((NX * NZ, NY * TOK, HALF), BF16),
        compiler_params=pltpu.CompilerParams(vmem_limit_bytes=32 * MIB),
    )(pieces)


def project_kernel(dcore, at_ref, rows, mine, theirs, out):
    low_y, core = at_ref[1], at_ref[2]
    for k, weight in enumerate((mine, theirs)):
        picked = []
        for dlow in range(2):
            head = lax.rem(low_y + dlow, 2) * 2 + lax.rem(core + dcore, 2)
            picked.append(weight[:, pl.ds(pl.multiple_of(head * HD, HD), HD)])
        terms = jnp.dot(
            rows[...], jnp.concatenate(picked, axis=1), preferred_element_type=F32)
        out[:, 2 * k * HD:2 * (k + 1) * HD] = terms.astype(out.dtype)


def project(dcore, at, rows, weight, theirs, dtype):
    count, width = rows.shape[0], theirs.shape[1]
    part = count // 4
    return pl.pallas_call(
        functools.partial(project_kernel, dcore),
        grid_spec=pltpu.PrefetchScalarGridSpec(
            num_scalar_prefetch=1,
            grid=(count // part,),
            in_specs=[
                pl.BlockSpec((part, HALF), lambda i, at: (i, 0)),
                pl.BlockSpec((HALF, width), lambda i, at: (at[0], 0)),
                pl.BlockSpec((HALF, width), lambda i, at: (0, 0)),
            ],
            out_specs=pl.BlockSpec((part, width), lambda i, at: (i, 0)),
        ),
        out_shape=jax.ShapeDtypeStruct((count, width), dtype),
        cost_estimate=pl.CostEstimate(
            flops=2 * count * HALF * width, transcendentals=0, bytes_accessed=4 * MIB),
        compiler_params=pltpu.CompilerParams(vmem_limit_bytes=32 * MIB),
    )(at, rows, weight, theirs)


def place_kernel(own, first, second, third, out):
    total = own[...] + first[...].astype(F32) + second[...].astype(F32) + third[...].astype(F32)
    total = total.astype(BF16)
    for x in range(NX):
        for z in range(NZ):
            for y in range(NY):
                begin = ((x * NZ + z) * NY + y) * TOK
                to = seq_of(x, y, z) * TOK
                out[to:to + TOK, :] = total[begin:begin + TOK]


def place(own, received):
    return pl.pallas_call(
        place_kernel,
        in_specs=[pl.BlockSpec(memory_space=pltpu.VMEM)] * 4,
        out_specs=pl.BlockSpec(memory_space=pltpu.VMEM),
        out_shape=jax.ShapeDtypeStruct(own.shape, BF16),
        compiler_params=pltpu.CompilerParams(vmem_limit_bytes=32 * MIB),
    )(own, *received)


def prepare_kernel(length_ref, keys, values, new_keys, new_values, meta, block):
    used = lax.broadcasted_iota(jnp.int32, (SLOTS, HD), 0) < length_ref[0]
    block[:SLOTS, :HD] = jnp.where(used, keys[...], keys[0:1, :])
    block[:SLOTS, HD:] = jnp.where(used, values[...], jnp.zeros((), BF16))
    block[SLOTS:SLOTS + TOK, :HD] = new_keys[...]
    block[SLOTS:SLOTS + TOK, HD:] = new_values[...]
    block[SLOTS + TOK:, :] = meta[...]


def prepare(length, *operands):
    return pl.pallas_call(
        prepare_kernel,
        in_specs=[pl.BlockSpec(memory_space=pltpu.SMEM)]
        + [pl.BlockSpec(memory_space=pltpu.VMEM)] * len(operands),
        out_specs=pl.BlockSpec(memory_space=pltpu.VMEM),
        out_shape=jax.ShapeDtypeStruct((SLOTS + 2 * TOK, 2 * HD), BF16),
        compiler_params=pltpu.CompilerParams(vmem_limit_bytes=60 * MIB),
    )(length, *operands)


def per_device(
    queries, new_keys, new_values, cache_keys, cache_values, cache_lengths, positions, out_weight
):
    y = lax.axis_index("seq") // NZ % NY
    head = lax.axis_index("head")

    length = cache_lengths[0]
    high, low = (positions // 32).astype(BF16), (positions % 32).astype(BF16)
    meta = jnp.concatenate([
        high[:, None], low[:, None],
        jnp.full((TOK, 1), (length // 64).astype(BF16)),
        jnp.full((TOK, 1), (length % 64).astype(BF16)),
        jnp.zeros((TOK, 2 * HD - 4), BF16)], axis=1)
    block = prepare(cache_lengths, cache_keys, cache_values, new_keys, new_values, meta)

    before, after = shift(block, dx=1), shift(block, dx=-1)
    block, queries, meta = lax.optimization_barrier((block, queries, meta))
    asking = jnp.concatenate([queries, meta[:, :HD]], axis=1)
    asking = jnp.broadcast_to(asking, (NY * NZ,) + asking.shape)
    asked = swap(asking, PLANES_YZ).reshape(GROUP, (HEADS + 1) * HD)
    far_head, far_tail = shift(before[:CUT], dx=1), shift(after[CUT:], dx=-1)

    other_rows = lax.dynamic_slice_in_dim(out_weight, (1 - y) * HALF, HALF)
    theirs = shift(other_rows, dy=1)

    near = [block, before, after]
    state = attend(asked, near, tuple((0, SLOTS, n) for n in range(3)))
    state, theirs = lax.optimization_barrier((state, theirs))
    partial = attend(
        asked, [far_head, far_tail], ((0, CUT, 3), (CUT, CUT, 3)), state, near + [far_tail])
    rows = swap(merge(swap(partial, PLANES_YZ)), PLANES_XZ).reshape(-1, HALF)

    at = jnp.stack([y, head // 2, head % 2]).astype(jnp.int32)
    sent = project(1, at, rows, out_weight, theirs, BF16)
    from_core = lax.ppermute(sent, "head", [(h, h ^ 1) for h in range(4)])
    terms = project(0, at, rows, out_weight, theirs, F32) + from_core.astype(F32)

    def across_y(value, dy, dlow):
        perm = [
            ((s * 4 + h), (s ^ (dy * NZ)) * 4 + (h ^ (dlow * 2)))
            for s in range(NX * NY * NZ) for h in range(4)]
        return lax.ppermute(value, ("seq", "head"), perm)

    others = [
        across_y(terms[:, k * HD:(k + 1) * HD].astype(BF16), k // 2, k % 2) for k in range(1, 4)]
    return place(terms[:, :HD], others)


def solution(mesh):
    return jax.shard_map(
        per_device,
        mesh=mesh,
        in_specs=(
            P("seq", "head"),
            P("seq", "head"),
            P("seq", "head"),
            P("seq", "head"),
            P("seq", "head"),
            P("seq"),
            P("seq"),
            P("head", "seq"),
        ),
        out_specs=P(None, ("seq", "head")),
        check_vma=False,
    )
```

```python
import functools
import math

import jax
import jax.numpy as jnp
from jax import lax
from jax.experimental import pallas as pl
from jax.experimental.pallas import tpu as pltpu
from jax.sharding import PartitionSpec as P

HD = 128
NX, NY, NZ = 4, 2, 4
SLOTS = 2048
TOK = 32
HEADS = 16
HALF = (HEADS // NY) * HD
PAY = HALF + HD
GROUP = NY * NZ * TOK
PAIRS = HEADS // 2
LANES = 2 * GROUP
DEPTH = HD + 16
CUT = SLOTS // 2
NEW0 = SLOTS
META0 = SLOTS + TOK
CHUNK = 512
PIECE = 128
HEADROOM = 2.0**60
TEMPER = math.log2(math.e) / math.sqrt(HD)
MIB = 2**20
BF16, F32 = jnp.bfloat16, jnp.float32


def seq_of(x, y, z):
    return ((x % NX) * NY + y % NY) * NZ + z % NZ


PLANES_YZ = [[seq_of(x, y, z) for y in range(NY) for z in range(NZ)] for x in range(NX)]
PLANES_XZ = [[seq_of(x, y, z) for x in range(NX) for z in range(NZ)] for y in range(NY)]


def swap(value, groups):
    return lax.all_to_all(value, "seq", 0, 0, axis_index_groups=groups, tiled=True)


def shift(value, dx=0, dy=0, dz=0):
    perm = [
        (seq_of(x, y, z), seq_of(x + dx, y + dy, z + dz))
        for x in range(NX)
        for y in range(NY)
        for z in range(NZ)
    ]
    return lax.ppermute(value, "seq", perm)


def attend_kernel(first, last, spans, q_ref, *rest):
    rest = list(rest)
    take = lambda n: [rest.pop(0) for _ in range(n)]
    asked_ref = take(1)[0] if last else None
    fresh_refs = take(4) if last else []
    refs = take(len(spans))
    top_in, acc_in = (None, None) if first else take(2)
    out_refs = take(1) if last else take(2)
    top_ref, acc_ref = take(2) if last else out_refs
    packed_keys, packed_values = take(2)

    def length_of(ref, row):
        meta = ref[row:row + 16, :].astype(F32)
        return (jnp.max(meta[:, 2:3]) * 64.0 + jnp.max(meta[:, 3:4])).astype(jnp.int32)

    def queries(pair):
        return jnp.concatenate(
            [q_ref[:, (2 * pair + j) * HD:(2 * pair + j + 1) * HD] for j in range(2)], axis=0)

    def score(keys, pair):
        return lax.dot_general(
            keys, queries(pair), (((1,), (1,)), ((), ())), preferred_element_type=F32)

    def chunk(i):
        at = pl.multiple_of(i * CHUNK, CHUNK)
        return packed_keys[pl.ds(at, CHUNK), :], packed_values[:, pl.ds(at, CHUNK)]

    if last:
        news = [ref[:TOK, :] for ref in fresh_refs]
        news = jnp.concatenate(news, axis=0)
        new_keys = news[:, :HD]
        new_values = jnp.concatenate(
            [news[:, HD:].T, jnp.ones((DEPTH - HD, NX * TOK), BF16)], axis=0)
        metas = [ref[TOK:, :] for ref in fresh_refs]
        metas = jnp.concatenate(metas, axis=0).astype(F32)
        given = metas[:, 0:1] * 32.0 + metas[:, 1:2]
        asked = asked_ref[...].astype(F32).T
        asked = asked[0:1] * 32.0 + asked[1:2]
        visible = given <= asked
        visible = jnp.concatenate([visible, visible], axis=1)

    lengths = [
        length_of(fresh_refs[holder], TOK) if last else length_of(refs[holder], META0)
        for _, _, holder in spans]

    count = jnp.int32(0)
    for ref, (begin, slots, _), length in zip(refs, spans, lengths):
        pieces = jnp.clip((length - begin + PIECE - 1) // PIECE, 0, slots // PIECE)

        def pack(i, _, ref=ref, begin=begin, length=length, count=count):
            to = pl.multiple_of((count + i) * PIECE, PIECE)
            piece = ref[pl.ds(pl.multiple_of(i * PIECE, PIECE), PIECE), :]
            packed_keys[pl.ds(to, PIECE), :] = piece[:, :HD]
            packed_values[:HD, pl.ds(to, PIECE)] = piece[:, HD:].T
            slot = lax.broadcasted_iota(jnp.int32, (DEPTH - HD, PIECE), 1) + begin + i * PIECE
            packed_values[HD:, pl.ds(to, PIECE)] = jnp.where(slot < length, 1.0, 0.0).astype(BF16)
            return 0

        lax.fori_loop(0, pieces, pack, 0)
        count = count + pieces
    chunks = (count * PIECE + CHUNK - 1) // CHUNK

    def fill(i, _):
        to = pl.multiple_of(i * PIECE, PIECE)
        packed_keys[pl.ds(to, PIECE), :] = packed_keys[:PIECE, :]
        packed_values[:, pl.ds(to, PIECE)] = jnp.zeros((DEPTH, PIECE), BF16)
        return 0

    lax.fori_loop(count, chunks * (CHUNK // PIECE), fill, 0)

    def loops(body, begin=0):
        def once(i, _):
            body(*chunk(i))
            return 0

        lax.fori_loop(begin, chunks, once, 0)

    if first:
        keys, values = chunk(0)
        scores = [score(keys, pair) for pair in range(PAIRS)]
        for pair, s in enumerate(scores):
            top = jnp.max(s, axis=0, keepdims=True)
            top_ref[pair] = top
            p = jnp.exp2((s - top) * TEMPER).astype(BF16)
            acc_ref[pair] = jnp.dot(values, p, preferred_element_type=F32)
    else:
        for pair in range(PAIRS):
            top = top_in[pair]
            top_ref[pair] = top
            s = score(new_keys, pair)
            p = jnp.where(visible, jnp.exp2((s - top) * TEMPER), 0.0).astype(BF16)
            acc_ref[pair] = acc_in[pair] + jnp.dot(new_values, p, preferred_element_type=F32)

    def add(keys, values):
        scores = [score(keys, pair) for pair in range(PAIRS)]
        for pair, s in enumerate(scores):
            p = jnp.exp2((s - top_ref[pair]) * TEMPER).astype(BF16)
            acc_ref[pair] += jnp.dot(values, p, preferred_element_type=F32)

    loops(add, 1 if first else 0)
    totals = jnp.concatenate([acc_ref[pair, HD:HD + 1, :] for pair in range(PAIRS)], axis=0)
    wild = jnp.where(totals < HEADROOM, 0.0, 1.0)

    @pl.when(jnp.max(wild) > 0.0)
    def _():
        for pair in range(PAIRS):
            top_ref[pair] = jnp.full((1, LANES), -1e30, F32) if first else top_in[pair]
            acc_ref[pair] = jnp.zeros((DEPTH, LANES), F32) if first else acc_in[pair]

        def raised(pair, s, values, seen):
            shown = s if seen is None else jnp.where(seen, s, -1e30)
            new = jnp.maximum(top_ref[pair], jnp.max(shown, axis=0, keepdims=True))
            p = jnp.exp2((s - new) * TEMPER)
            p = (p if seen is None else jnp.where(seen, p, 0.0)).astype(BF16)
            keep = jnp.exp2((top_ref[pair] - new) * TEMPER)
            acc_ref[pair] = acc_ref[pair] * keep + jnp.dot(values, p, preferred_element_type=F32)
            top_ref[pair] = new

        def careful(keys, values):
            for pair in range(PAIRS):
                raised(pair, score(keys, pair), values, None)

        loops(careful)
        if last:
            for pair in range(PAIRS):
                raised(pair, score(new_keys, pair), new_values, visible)

    if last:
        out = out_refs[0]
        for half in range(NY):
            levels = []
            for pair in range(half * PAIRS // 2, (half + 1) * PAIRS // 2):
                total = acc_ref[pair, HD:HD + 1, :]
                level = top_ref[pair] * TEMPER + jnp.log2(total)
                part = (acc_ref[pair, :HD, :] * (1.0 / total)).astype(BF16)
                for j in range(2):
                    levels.append(level[:, j * GROUP:(j + 1) * GROUP])
                    block = part[:, j * GROUP:(j + 1) * GROUP].T
                    at = (2 * pair + j) * HD - half * HALF
                    for z in range(NZ):
                        for y in range(NY):
                            rows = y * NZ * TOK + z * TOK
                            out[half * NZ + z, y * TOK:(y + 1) * TOK, at:at + HD] = (
                                block[rows:rows + TOK])
            level = jnp.concatenate(levels, axis=0)
            high = level.astype(BF16).astype(F32)
            middle = (level - high).astype(BF16).astype(F32)
            low = level - high - middle
            block = jnp.concatenate(
                [high, middle, low, jnp.zeros((HD - 24, GROUP), F32)], axis=0).T.astype(BF16)
            for z in range(NZ):
                for y in range(NY):
                    rows = y * NZ * TOK + z * TOK
                    out[half * NZ + z, y * TOK:(y + 1) * TOK, HALF:] = block[rows:rows + TOK]


def attend(asked, blocks, spans, state=None, fresh=None):
    first, last = state is None, fresh is not None
    operands = [asked] + ([asked] + list(fresh) if last else []) + list(blocks) + list(state or ())
    whole = lambda array: pl.BlockSpec(array.shape, lambda i: (0,) * array.ndim)
    specs = [pl.BlockSpec((GROUP, HEADS * HD), lambda i: (0, 0))]
    if last:
        specs += [pl.BlockSpec((GROUP, HD), lambda i: (0, HEADS))]
        end = lambda array: array.shape[0] // (2 * TOK) - 1
        specs += [
            pl.BlockSpec((2 * TOK, 2 * HD), functools.partial(lambda n, i: (n, 0), end(array)))
            for array in fresh]
    specs += [whole(operand) for operand in operands[len(specs):]]
    held = [
        jax.ShapeDtypeStruct((PAIRS, 1, LANES), F32),
        jax.ShapeDtypeStruct((PAIRS, DEPTH, LANES), F32)]
    results = [jax.ShapeDtypeStruct((NY * NZ, NY * TOK, PAY), BF16)] if last else held
    scratch = [pltpu.VMEM(h.shape, F32) for h in held] if last else []
    keys = sum(slots for _, slots, _ in spans)
    out = pl.pallas_call(
        functools.partial(attend_kernel, first, last, spans),
        grid=(1,),
        in_specs=specs,
        out_specs=[whole(result) for result in results],
        out_shape=results,
        scratch_shapes=scratch + [
            pltpu.VMEM((keys, HD), BF16),
            pltpu.VMEM((DEPTH, keys), BF16)],
        cost_estimate=pl.CostEstimate(
            flops=4 * HEADS * GROUP * HD * keys, transcendentals=HEADS * GROUP * keys,
            bytes_accessed=4 * MIB),
        compiler_params=pltpu.CompilerParams(vmem_limit_bytes=40 * MIB),
    )(*operands)
    return out[0] if last else out


def merge_kernel(pieces, out):
    count = NY * NZ
    split = [pieces[r, :, HALF:].astype(F32) for r in range(count)]
    levels = [term[:, 0:8] + term[:, 8:16] + term[:, 16:24] for term in split]
    top = functools.reduce(jnp.maximum, levels)
    shares = [jnp.exp2(level - top) for level in levels]
    whole = functools.reduce(jnp.add, shares)
    for j in range(HALF // HD):
        total = jnp.zeros((NY * TOK, HD), F32)
        for r in range(count):
            total += shares[r][:, j:j + 1] * pieces[r, :, j * HD:(j + 1) * HD].astype(F32)
        merged = (total / whole[:, j:j + 1]).astype(BF16)
        for to in range(NX * NZ):
            out[to, :, j * HD:(j + 1) * HD] = merged


def merge(pieces):
    return pl.pallas_call(
        merge_kernel,
        in_specs=[pl.BlockSpec(memory_space=pltpu.VMEM)],
        out_specs=pl.BlockSpec(memory_space=pltpu.VMEM),
        out_shape=jax.ShapeDtypeStruct((NX * NZ, NY * TOK, HALF), BF16),
        compiler_params=pltpu.CompilerParams(vmem_limit_bytes=32 * MIB),
    )(pieces)


def project_kernel(dcore, at_ref, rows, mine, theirs, out):
    low_y, core = at_ref[1], at_ref[2]
    for k, weight in enumerate((mine, theirs)):
        picked = []
        for dlow in range(2):
            head = lax.rem(low_y + dlow, 2) * 2 + lax.rem(core + dcore, 2)
            picked.append(weight[:, pl.ds(pl.multiple_of(head * HD, HD), HD)])
        terms = jnp.dot(
            rows[...], jnp.concatenate(picked, axis=1), preferred_element_type=F32)
        out[:, 2 * k * HD:2 * (k + 1) * HD] = terms.astype(out.dtype)


def project(dcore, at, rows, weight, theirs, dtype):
    count, width = rows.shape[0], theirs.shape[1]
    part = count // 4
    return pl.pallas_call(
        functools.partial(project_kernel, dcore),
        grid_spec=pltpu.PrefetchScalarGridSpec(
            num_scalar_prefetch=1,
            grid=(count // part,),
            in_specs=[
                pl.BlockSpec((part, HALF), lambda i, at: (i, 0)),
                pl.BlockSpec((HALF, width), lambda i, at: (at[0], 0)),
                pl.BlockSpec((HALF, width), lambda i, at: (0, 0)),
            ],
            out_specs=pl.BlockSpec((part, width), lambda i, at: (i, 0)),
        ),
        out_shape=jax.ShapeDtypeStruct((count, width), dtype),
        cost_estimate=pl.CostEstimate(
            flops=2 * count * HALF * width, transcendentals=0, bytes_accessed=4 * MIB),
        compiler_params=pltpu.CompilerParams(vmem_limit_bytes=32 * MIB),
    )(at, rows, weight, theirs)


def place_kernel(own, first, second, third, out):
    total = own[...] + first[...].astype(F32) + second[...].astype(F32) + third[...].astype(F32)
    total = total.astype(BF16)
    for x in range(NX):
        for z in range(NZ):
            for y in range(NY):
                begin = ((x * NZ + z) * NY + y) * TOK
                to = seq_of(x, y, z) * TOK
                out[to:to + TOK, :] = total[begin:begin + TOK]


def place(own, received):
    return pl.pallas_call(
        place_kernel,
        in_specs=[pl.BlockSpec(memory_space=pltpu.VMEM)] * 4,
        out_specs=pl.BlockSpec(memory_space=pltpu.VMEM),
        out_shape=jax.ShapeDtypeStruct(own.shape, BF16),
        compiler_params=pltpu.CompilerParams(vmem_limit_bytes=32 * MIB),
    )(own, *received)


def prepare_kernel(length_ref, keys, values, new_keys, new_values, meta, block):
    used = lax.broadcasted_iota(jnp.int32, (SLOTS, HD), 0) < length_ref[0]
    block[:SLOTS, :HD] = jnp.where(used, keys[...], keys[0:1, :])
    block[:SLOTS, HD:] = jnp.where(used, values[...], jnp.zeros((), BF16))
    block[SLOTS:SLOTS + TOK, :HD] = new_keys[...]
    block[SLOTS:SLOTS + TOK, HD:] = new_values[...]
    block[SLOTS + TOK:, :] = meta[...]


def prepare(length, *operands):
    return pl.pallas_call(
        prepare_kernel,
        in_specs=[pl.BlockSpec(memory_space=pltpu.SMEM)]
        + [pl.BlockSpec(memory_space=pltpu.VMEM)] * len(operands),
        out_specs=pl.BlockSpec(memory_space=pltpu.VMEM),
        out_shape=jax.ShapeDtypeStruct((SLOTS + 2 * TOK, 2 * HD), BF16),
        compiler_params=pltpu.CompilerParams(vmem_limit_bytes=60 * MIB),
    )(length, *operands)


def per_device(
    queries, new_keys, new_values, cache_keys, cache_values, cache_lengths, positions, out_weight
):
    y = lax.axis_index("seq") // NZ % NY
    head = lax.axis_index("head")

    length = cache_lengths[0]
    high, low = (positions // 32).astype(BF16), (positions % 32).astype(BF16)
    meta = jnp.concatenate([
        high[:, None], low[:, None],
        jnp.full((TOK, 1), (length // 64).astype(BF16)),
        jnp.full((TOK, 1), (length % 64).astype(BF16)),
        jnp.zeros((TOK, 2 * HD - 4), BF16)], axis=1)
    block = prepare(cache_lengths, cache_keys, cache_values, new_keys, new_values, meta)

    before, after = shift(block, dx=1), shift(block, dx=-1)
    block, queries, meta = lax.optimization_barrier((block, queries, meta))
    asking = jnp.concatenate([queries, meta[:, :HD]], axis=1)
    asking = jnp.broadcast_to(asking, (NY * NZ,) + asking.shape)
    asked = swap(asking, PLANES_YZ).reshape(GROUP, (HEADS + 1) * HD)
    far_head, far_tail = shift(before[:CUT], dx=1), shift(after[CUT:], dx=-1)

    other_rows = lax.dynamic_slice_in_dim(out_weight, (1 - y) * HALF, HALF)
    theirs = shift(other_rows, dy=1)

    near = [block, before, after]
    state = attend(asked, near, tuple((0, SLOTS, n) for n in range(3)))
    state, theirs = lax.optimization_barrier((state, theirs))
    partial = attend(
        asked, [far_head, far_tail], ((0, CUT, 3), (CUT, CUT, 3)), state, near + [far_tail])
    rows = swap(merge(swap(partial, PLANES_YZ)), PLANES_XZ).reshape(-1, HALF)

    at = jnp.stack([y, head // 2, head % 2]).astype(jnp.int32)
    sent = project(1, at, rows, out_weight, theirs, BF16)
    from_core = lax.ppermute(sent, "head", [(h, h ^ 1) for h in range(4)])
    terms = project(0, at, rows, out_weight, theirs, F32) + from_core.astype(F32)

    def across_y(value, dy, dlow):
        perm = [
            ((s * 4 + h), (s ^ (dy * NZ)) * 4 + (h ^ (dlow * 2)))
            for s in range(NX * NY * NZ) for h in range(4)]
        return lax.ppermute(value, ("seq", "head"), perm)

    others = [
        across_y(terms[:, k * HD:(k + 1) * HD].astype(BF16), k // 2, k % 2) for k in range(1, 4)]
    return place(terms[:, :HD], others)


def solution(mesh):
    return jax.shard_map(
        per_device,
        mesh=mesh,
        in_specs=(
            P("seq", "head"),
            P("seq", "head"),
            P("seq", "head"),
            P("seq", "head"),
            P("seq", "head"),
            P("seq"),
            P("seq"),
            P("head", "seq"),
        ),
        out_specs=P(None, ("seq", "head")),
        check_vma=False,
    )
```
